32 devices in a mesh: seq: 4 (over y, x), tensor: 8 (over z, core).
Axes of the slice: x: 2, y: 2, z: 4, core: 2. Of those that a mesh axis runs over, the one named last changes fastest.
Arguments:
- inputs: bfloat16 [768, 8192], P(('seq', 'tensor')), may hold values from -6 to 6
- grad_out: bfloat16 [768, 8192], P(('seq', 'tensor')), may hold values from -6 to 6
- up_blocks: bfloat16 [224, 8, 128, 128], P('tensor'), may hold values from -0.1875 to 0.1875
- up_index: int32 [224, 8], P('tensor'), may hold values from 0 to 63, as said below
- down_blocks: bfloat16 [224, 8, 128, 128], P('tensor'), may hold values from -0.1875 to 0.1875
- down_index: int32 [224, 8], P('tensor'), may hold values from 0 to 63, as said below
Outputs:
- grad_in: bfloat16 [768, 8192], P(('seq', 'tensor'))
- grad_up: bfloat16 [224, 8, 128, 128], P('tensor', None, 'seq')
- grad_down: bfloat16 [224, 8, 128, 128], P('tensor', None, 'seq')
The draws below stay inside these ranges and needn't reach their ends.
Inputs may be any that keep to these rules, and one draw needn't show every extreme that they name: `up_index`: in every row the 8 block numbers are different, and every number from 0 to 63 appears in some row. `down_index`: in every row the 8 block numbers are different, and every number from 0 to 63 appears in some row.
All inputs are finite; a program needn't handle non-finite values.
Results may differ from the reference program's by a relative error of at most 0.012.
Values may be sent and summed in bfloat16 or wider, within the bound.
A program may use at most 128 MiB of HBM per device.

```python
import math
import jax
import jax.numpy as jnp
from jax import lax

D = 8192
BS = 128
K = 8
TOK_SEQ = 192
NDB = 64
NBH = 224
TOKENS = 768
N_SEQ = 4
N_TENSOR = 8


def mask_offsets():
    values = [0]
    power = 1
    while power < NDB:
        values.append(power)
        power = power * 2
    if NDB - 1 not in values:
        values.append(NDB - 1)
    for extra in range(NDB):
        if extra not in values:
            values.append(extra)
    return values[:K]


def butterfly_index(key):
    relabel = jax.random.permutation(jax.random.fold_in(key, 11), NDB).astype(jnp.int32)
    offset = jax.random.randint(jax.random.fold_in(key, 12), (), 0, NDB, dtype=jnp.int32)
    masks = jnp.array(mask_offsets(), dtype=jnp.int32)
    base = (jnp.arange(NBH, dtype=jnp.int32) + offset) % NDB
    return relabel[jnp.bitwise_xor(base[:, None], masks[None, :])]


def draw_up_index(key, part):
    key = jax.random.fold_in(key, 3)
    return butterfly_index(key)


def draw_down_index(key, part):
    key = jax.random.fold_in(key, 5)
    return butterfly_index(key)


def level_of(stream_key, dims, pieces, smallest, largest):
    loudness, own = 1.0, jax.random.fold_in(stream_key, 6)
    for position, shards_of in pieces:
        draws = jnp.exp(jax.random.uniform(jax.random.fold_in(own, position), (shards_of,), jnp.float32, smallest / len(pieces), largest / len(pieces)))
        loudness = loudness * jnp.repeat(draws, dims[position] // shards_of).reshape([-1 if axis == position else 1 for axis in range(len(dims))])
    return loudness


def gaussian(stream_key, extent, scale, reach, split=(), held_as=jnp.bfloat16):
    entries = scale * jax.random.normal(stream_key, extent, jnp.float32)
    if split:
        entries = entries * level_of(stream_key, extent, split, -0.22, 0.18)
    return jnp.clip(entries, -reach, reach).astype(held_as)


def setup_inputs(seed: int = 0) -> dict:
    seeds = jax.random.split(jax.random.key(seed), 7)
    return {
        "inputs": gaussian(seeds[0], (TOKENS, D), 1.0, 6.0, ((0, 32),)),
        "grad_out": gaussian(seeds[1], (TOKENS, D), 1.0, 6.0, ((0, 32),)),
        "up_blocks": gaussian(seeds[2], (NBH, K, BS, BS), (K * BS) ** -0.5, 0.1875, ((0, 8),)),
        "up_index": draw_up_index(jax.random.fold_in(seeds[6], 71), 0),
        "down_blocks": gaussian(seeds[4], (NBH, K, BS, BS), (K * BS) ** -0.5, 0.1875, ((0, 8),)),
        "down_index": draw_down_index(jax.random.fold_in(seeds[6], 71), 0),
    }


def reference(inputs, grad_out, up_blocks, up_index, down_blocks, down_index):
    blocks_wide = D // BS
    local_blocks = NBH // N_TENSOR
    factor = 1.0 / math.sqrt(TOKENS)
    grouped_in = inputs.reshape(N_SEQ, TOK_SEQ, blocks_wide, BS)
    grouped_grad = grad_out.reshape(N_SEQ, TOK_SEQ, blocks_wide, BS)

    def one_group(totals, stacked):
        up_now, up_where, down_now, down_where = stacked
        up_where = up_where.astype(jnp.int32)
        down_where = down_where.astype(jnp.int32)
        picked = jnp.take(grouped_in, up_where, axis=2).astype(jnp.float32)
        picked_grad = jnp.take(grouped_grad, down_where, axis=2).astype(jnp.float32)
        up_float = up_now.astype(jnp.float32)
        preact = jnp.einsum('srjkc,jkch->srjh', picked, up_float)
        hidden_grad = jnp.einsum('srjko,jkho->srjh', picked_grad, down_now.astype(jnp.float32))
        gating = jax.nn.sigmoid(preact)
        activated = (preact * gating).astype(jnp.bfloat16).astype(jnp.float32)
        preact_grad = (hidden_grad * gating * (1.0 + preact * (1.0 - gating))).astype(jnp.bfloat16).astype(jnp.float32)
        up_part = (jnp.einsum('srjkc,srjh->sjkch', picked, preact_grad) * factor).astype(jnp.bfloat16)
        down_part = (jnp.einsum('srjh,srjko->sjkho', activated, picked_grad) * factor).astype(jnp.bfloat16)
        grad_up = lax.optimization_barrier(jnp.sum(up_part.astype(jnp.float32), axis=0)).astype(jnp.bfloat16)
        grad_down = lax.optimization_barrier(jnp.sum(down_part.astype(jnp.float32), axis=0)).astype(jnp.bfloat16)
        contrib = jnp.einsum('srjh,jkch->srjkc', preact_grad, up_float)
        contrib = contrib.reshape(N_SEQ, TOK_SEQ, local_blocks * K, BS)
        partial_value = jnp.zeros((N_SEQ, TOK_SEQ, blocks_wide, BS), jnp.float32)
        partial_value = partial_value.at[:, :, up_where.reshape(-1)].add(contrib)
        partial_value = partial_value.astype(jnp.bfloat16).astype(jnp.float32)
        return (totals + partial_value, (grad_up, grad_down))
    stacked = (up_blocks.reshape(N_TENSOR, local_blocks, K, BS, BS), up_index.reshape(N_TENSOR, local_blocks, K), down_blocks.reshape(N_TENSOR, local_blocks, K, BS, BS), down_index.reshape(N_TENSOR, local_blocks, K))
    initial = jnp.zeros((N_SEQ, TOK_SEQ, blocks_wide, BS), jnp.float32)
    totals, grads = lax.scan(one_group, initial, stacked)
    grad_in = totals.astype(jnp.bfloat16).reshape(TOKENS, D)
    grad_up = grads[0].reshape(NBH, K, BS, BS)
    grad_down = grads[1].reshape(NBH, K, BS, BS)
    return (grad_in, grad_up, grad_down)
```

```python
import functools
import math

import jax
import jax.numpy as jnp
from jax import lax
from jax.experimental import pallas as pl
from jax.experimental.pallas import tpu as pltpu
from jax.sharding import PartitionSpec as P

MESH = pl.DeviceIdType.MESH
MIB = 1024 * 1024


def gather_kernel(
    zs, in_ref, go_ref, out, loc, own_send, own_recv, recv, zsend, xysend, hsend, sib_send, sib_recv
):
    s, t = lax.axis_index("seq"), lax.axis_index("tensor")
    z, c = t // 2, t % 2
    x, y = s % 2, s // 2
    xn, yn, dg = y * 2 + (1 - x), (1 - y) * 2 + x, (1 - y) * 2 + (1 - x)
    sib = z * 2 + (1 - c)

    barrier = pltpu.get_barrier_semaphore()
    for dev in ((s, sib), (xn, t), (yn, t)):
        pl.semaphore_signal(barrier, inc=1, device_id=dev, device_id_type=MESH)

    @pl.when(z < zs - 1)
    def _():
        pl.semaphore_signal(barrier, inc=1, device_id=(s, t + 2), device_id_type=MESH)

    @pl.when(z > 0)
    def _():
        pl.semaphore_signal(barrier, inc=1, device_id=(s, t - 2), device_id_type=MESH)

    pl.semaphore_wait(barrier, 3 + jnp.minimum(z, 1) + jnp.minimum(zs - 1 - z, 1))

    def copy(ref, send, recv_sem, dev):
        return pltpu.make_async_remote_copy(
            src_ref=ref, dst_ref=ref, send_sem=send, recv_sem=recv_sem, device_id=dev, device_id_type=MESH
        )

    def own_copy(a, ref):
        return pltpu.make_async_remote_copy(
            src_ref=ref,
            dst_ref=out.at[a, s, z, c],
            send_sem=own_send.at[a],
            recv_sem=own_recv.at[a],
            device_id=(s, sib),
            device_id_type=MESH,
        )

    def unit(q, o):
        return out.at[c, q, o]

    def right(o):
        return copy(unit(s, o), zsend.at[0, o], recv.at[s, o, 0], (s, t + 2))

    def left(o):
        return copy(unit(s, o), zsend.at[1, o], recv.at[s, o, 0], (s, t - 2))

    def to_x(o):
        return copy(unit(s, o), xysend.at[0, o], recv.at[s, o, 0], (xn, t))

    def to_y(o):
        return copy(unit(s, o), xysend.at[1, o], recv.at[s, o, 0], (yn, t))

    def half_y(o):
        return copy(out.at[c, xn, o, 0], hsend.at[0, o], recv.at[xn, o, 0], (yn, t))

    def half_x(o):
        return copy(out.at[c, yn, o, 1], hsend.at[1, o], recv.at[yn, o, 1], (xn, t))

    def to_sib(q, o):
        return copy(unit(q, o), sib_send.at[q, o], sib_recv.at[q, o], (s, sib))

    def from_sib(q, o):
        return copy(out.at[1 - c, q, o], sib_send.at[q, o], sib_recv.at[q, o], (s, sib))

    def got(q, o):
        copy(unit(q, o), xysend.at[0, o], recv.at[q, o, 0], (xn, t)).wait_recv()

    def got_half(o, h):
        copy(out.at[c, dg, o, h], hsend.at[h, o], recv.at[dg, o, h], (xn, t)).wait_recv()

    def spread(o):
        to_x(o).start()
        to_y(o).start()

    def from_xy(o):
        got(xn, o)
        half_y(o).start()
        to_sib(xn, o).start()
        got(yn, o)
        half_x(o).start()
        to_sib(yn, o).start()

    def from_diagonal(o):
        got_half(o, 0)
        got_half(o, 1)
        to_sib(dg, o).start()

    def at_distance(d, act):
        if d == 0:
            act(z)
            return
        pl.when(z - d >= 0)(lambda: act(z - d))
        pl.when(z + d < zs)(lambda: act(z + d))

    locals_ = [
        pltpu.make_async_copy(ref, out.at[a, s, z, c], loc.at[a]) for a, ref in enumerate((in_ref, go_ref))
    ]
    owns = [own_copy(a, ref) for a, ref in enumerate((in_ref, go_ref))]
    for one in owns + locals_:
        one.start()
    for one in locals_:
        one.wait()
    for one in owns:
        one.wait_recv()

    pl.when(z < zs - 1)(lambda: right(z).start())
    pl.when(z > 0)(lambda: left(z).start())
    spread(z)
    for d in range(1, zs):

        @pl.when(z - d >= 0)
        def _(d=d):
            o = z - d
            got(s, o)
            pl.when(z < zs - 1)(lambda: right(o).start())
            spread(o)
            to_sib(s, o).start()

        @pl.when(z + d < zs)
        def _(d=d):
            o = z + d
            got(s, o)
            pl.when(z > 0)(lambda: left(o).start())
            spread(o)
            to_sib(s, o).start()

        at_distance(d - 1, from_xy)
        if d >= 2:
            at_distance(d - 2, from_diagonal)
    at_distance(zs - 1, from_xy)
    if zs >= 2:
        at_distance(zs - 2, from_diagonal)
    at_distance(zs - 1, from_diagonal)

    for one in owns:
        one.wait_send()
    for o in range(zs):
        pl.when((o <= z) & (z < zs - 1))(lambda o=o: right(o).wait_send())
        pl.when((o >= z) & (z > 0))(lambda o=o: left(o).wait_send())
        to_x(o).wait_send()
        to_y(o).wait_send()
        half_y(o).wait_send()
        half_x(o).wait_send()
        for q in (xn, yn, dg):
            to_sib(q, o).wait_send()
            from_sib(q, o).wait_recv()

        @pl.when(z != o)
        def _(o=o):
            to_sib(s, o).wait_send()
            from_sib(s, o).wait_recv()


def gather_all(inputs, grad_out, seqs, zs):
    rows, features = inputs.shape
    dma = pltpu.SemaphoreType.DMA
    return pl.pallas_call(
        functools.partial(gather_kernel, zs),
        out_shape=jax.ShapeDtypeStruct((2, seqs, zs, 2, rows, features), inputs.dtype),
        in_specs=[pl.BlockSpec(memory_space=pl.ANY)] * 2,
        out_specs=pl.BlockSpec(memory_space=pl.ANY),
        scratch_shapes=[
            dma((2,)),
            dma((2,)),
            dma((2,)),
            dma((seqs, zs, 2)),
            dma((2, zs)),
            dma((2, zs)),
            dma((2, zs)),
            dma((seqs, zs)),
            dma((seqs, zs)),
        ],
        compiler_params=pltpu.CompilerParams(collective_id=0, has_side_effects=True),
        name="gather_all",
    )(inputs, grad_out)


def picked_blocks(ref, index, j, slots, width):
    return jnp.concatenate(
        [ref[:, pl.ds(pl.multiple_of(index[j, k] * width, width), width)] for k in range(slots)], axis=1
    )


def forward(xs, gs, up, down):
    slots, width, _ = up.shape
    preact = jnp.dot(xs, up.reshape(slots * width, width), preferred_element_type=jnp.float32)
    down_wide = jnp.concatenate([down[k] for k in range(slots)], axis=1)
    hidden_grad = lax.dot_general(
        gs, down_wide, (((1,), (1,)), ((), ())), preferred_element_type=jnp.float32
    )
    gating = jax.nn.sigmoid(preact)
    pg = (hidden_grad * gating * (1.0 + preact * (1.0 - gating))).astype(jnp.bfloat16)
    return (preact * gating).astype(jnp.bfloat16), pg


def input_kernel(ui, di, pos, x_ref, g_ref, up_ref, down_ref, out_ref, acc):
    j = pl.program_id(0)
    slots, width = up_ref.shape[1], up_ref.shape[2]

    @pl.when(j == 0)
    def _():
        acc[...] = jnp.zeros_like(acc)

    xs = picked_blocks(x_ref, ui, j, slots, width)
    gs = picked_blocks(g_ref, di, j, slots, width)
    up = up_ref[0]
    _, pg = forward(xs, gs, up, down_ref[0])
    terms = lax.dot_general(
        pg, up.reshape(slots * width, width), (((1,), (1,)), ((), ())), preferred_element_type=jnp.float32
    )
    for k in range(slots):
        where = pl.ds(pl.multiple_of(ui[j, k] * width, width), width)
        acc[:, where] += terms[:, k * width : (k + 1) * width]

    @pl.when(j == pl.num_programs(0) - 1)
    def _():
        out_ref[...] = acc[...].astype(out_ref.dtype)


def input_part(up_index, down_index, pos, both, up_blocks, down_blocks, rows):
    count, slots, width, _ = up_blocks.shape
    features = both.shape[2]
    weight = pl.BlockSpec((1, slots, width, width), lambda j, *_: (j, 0, 0, 0))
    return pl.pallas_call(
        input_kernel,
        out_shape=jax.ShapeDtypeStruct((rows, features), both.dtype),
        grid_spec=pltpu.PrefetchScalarGridSpec(
            num_scalar_prefetch=3,
            grid=(count,),
            in_specs=[
                pl.BlockSpec(
                    (None, rows, features), lambda j, ui, di, pos: (0, pos[0], 0), pipeline_mode=pl.Buffered(1)
                ),
                pl.BlockSpec(
                    (None, rows, features), lambda j, ui, di, pos: (1, pos[0], 0), pipeline_mode=pl.Buffered(1)
                ),
                weight,
                weight,
            ],
            out_specs=pl.BlockSpec((rows, features), lambda j, *_: (0, 0), pipeline_mode=pl.Buffered(1)),
            scratch_shapes=[pltpu.VMEM((rows, features), jnp.float32)],
        ),
        compiler_params=pltpu.CompilerParams(vmem_limit_bytes=40 * MIB),
        cost_estimate=pl.CostEstimate(
            flops=6 * rows * count * slots * width * width,
            bytes_accessed=4 * count * slots * width * width + 6 * rows * features,
            transcendentals=rows * count * width,
        ),
        name="input_part",
    )(up_index, down_index, pos, both, both, up_blocks, down_blocks)


def grads_kernel(factor, ui, di, pos, x_ref, g_ref, up_ref, down_ref, gup_ref, gdown_ref, xq, turned):
    j = pl.program_id(0)
    slots, width = up_ref.shape[1], up_ref.shape[2]
    share = gup_ref.shape[2]
    mine = pl.ds(pl.multiple_of(pos[0] * share, share), share)

    @pl.when(j == 0)
    def _():
        def one(b, carry):
            turned[...] = x_ref[:, pl.ds(pl.multiple_of(b * width, width), width)].T
            xq[b] = turned[mine, :]
            return carry

        lax.fori_loop(0, xq.shape[0], one, 0)

    xs = picked_blocks(x_ref, ui, j, slots, width)
    gs = picked_blocks(g_ref, di, j, slots, width)
    activated, pg = forward(xs, gs, up_ref[0], down_ref[0])
    quarter = jnp.concatenate([xq[ui[j, k]] for k in range(slots)], axis=0)
    gup = jnp.dot(quarter, pg, preferred_element_type=jnp.float32) * factor
    gup_ref[0] = gup.astype(gup_ref.dtype).reshape(slots, share, width)
    turned[...] = activated.T
    gdown = jnp.dot(turned[mine, :], gs, preferred_element_type=jnp.float32) * factor
    for k in range(slots):
        gdown_ref[0, k] = gdown[:, k * width : (k + 1) * width].astype(gdown_ref.dtype)


def block_grads(up_index, down_index, pos, both, up_blocks, down_blocks, share, factor):
    count, slots, width, _ = up_blocks.shape
    _, tokens, features = both.shape
    weight = pl.BlockSpec((1, slots, width, width), lambda j, *_: (j, 0, 0, 0))
    result = pl.BlockSpec((1, slots, share, width), lambda j, *_: (j, 0, 0, 0))
    shape = jax.ShapeDtypeStruct((count, slots, share, width), both.dtype)
    return pl.pallas_call(
        functools.partial(grads_kernel, factor),
        out_shape=[shape, shape],
        grid_spec=pltpu.PrefetchScalarGridSpec(
            num_scalar_prefetch=3,
            grid=(count,),
            in_specs=[
                pl.BlockSpec((None, tokens, features), lambda j, *_: (0, 0, 0), pipeline_mode=pl.Buffered(1)),
                pl.BlockSpec((None, tokens, features), lambda j, *_: (1, 0, 0), pipeline_mode=pl.Buffered(1)),
                weight,
                weight,
            ],
            out_specs=[result, result],
            scratch_shapes=[
                pltpu.VMEM((features // width, share, tokens), both.dtype),
                pltpu.VMEM((width, tokens), both.dtype),
            ],
        ),
        compiler_params=pltpu.CompilerParams(vmem_limit_bytes=56 * MIB),
        cost_estimate=pl.CostEstimate(
            flops=6 * tokens * count * slots * width * width,
            bytes_accessed=6 * count * slots * width * width + 4 * tokens * features,
            transcendentals=tokens * count * width,
        ),
        name="block_grads",
    )(up_index, down_index, pos, both, both, up_blocks, down_blocks)


def local_all_tokens(inputs, grad_out, up_blocks, up_index, down_blocks, down_index):
    tensor_count = lax.axis_size("tensor")
    seq_count = lax.axis_size("seq")
    rows_here, features = inputs.shape
    block = up_blocks.shape[2]
    group_rows = rows_here * tensor_count
    factor = 1.0 / math.sqrt(group_rows * seq_count)
    both = gather_all(inputs, grad_out, seq_count, tensor_count // 2)
    both = both.reshape(2, group_rows * seq_count, features)
    pos = lax.axis_index("seq").astype(jnp.int32).reshape(1)
    part = input_part(up_index, down_index, pos, both, up_blocks, down_blocks, group_rows)
    pieces = part.reshape(tensor_count, rows_here, features)
    received = lax.all_to_all(pieces, "tensor", split_axis=0, concat_axis=0, tiled=True)
    grad_up, grad_down = block_grads(
        up_index, down_index, pos, both, up_blocks, down_blocks, block // seq_count, factor
    )
    grad_in = jnp.sum(received.astype(jnp.float32), axis=0).astype(jnp.bfloat16)
    return (grad_in, grad_up, grad_down)


def local(inputs, grad_out, up_blocks, up_index, down_blocks, down_index):
    tensor_count = lax.axis_size("tensor")
    seq_count = lax.axis_size("seq")
    rows_here, features = inputs.shape
    local_blocks, slots, block, _ = up_blocks.shape
    blocks_wide = features // block
    group_rows = rows_here * tensor_count
    factor = 1.0 / math.sqrt(group_rows * seq_count)
    flat_index = up_index.reshape(-1)
    in_rows = lax.all_gather(inputs, "tensor", axis=0, tiled=True)
    grad_rows = lax.all_gather(grad_out, "tensor", axis=0, tiled=True)
    piece_rows = in_rows.shape[0]
    picked = jnp.take(in_rows.reshape(piece_rows, blocks_wide, block), up_index, axis=1)
    picked_grad = jnp.take(grad_rows.reshape(piece_rows, blocks_wide, block), down_index, axis=1)
    preact = jnp.einsum("rjkc,jkch->rjh", picked, up_blocks, preferred_element_type=jnp.float32)
    hidden_grad = jnp.einsum(
        "rjko,jkho->rjh", picked_grad, down_blocks, preferred_element_type=jnp.float32
    )
    gating = jax.nn.sigmoid(preact)
    activated = (preact * gating).astype(jnp.bfloat16)
    preact_grad = (hidden_grad * gating * (1.0 + preact * (1.0 - gating))).astype(jnp.bfloat16)
    up_sum = jnp.einsum("rjkc,rjh->jkch", picked, preact_grad, preferred_element_type=jnp.float32)
    down_sum = jnp.einsum(
        "rjh,rjko->jkho", activated, picked_grad, preferred_element_type=jnp.float32
    )
    contrib = jnp.einsum(
        "rjh,jkch->rjkc", preact_grad, up_blocks, preferred_element_type=jnp.float32
    )
    contrib = contrib.reshape(piece_rows, local_blocks * slots, block)
    partial_value = (
        jnp.zeros((piece_rows, blocks_wide, block), jnp.float32).at[:, flat_index].add(contrib)
    )
    input_grad = partial_value
    up_sum, down_sum, input_grad = (up_sum, down_sum, input_grad)
    share = block // seq_count
    up_part = (
        (up_sum * factor).astype(jnp.bfloat16).reshape(local_blocks, slots, seq_count, share, block)
    )
    down_part = (
        (down_sum * factor)
        .astype(jnp.bfloat16)
        .reshape(local_blocks, slots, seq_count, share, block)
    )
    up_recv, down_recv = (
        lax.all_to_all(up_part, "seq", split_axis=2, concat_axis=2, tiled=True),
        lax.all_to_all(down_part, "seq", split_axis=2, concat_axis=2, tiled=True),
    )
    grad_up = jnp.sum(up_recv.astype(jnp.float32), axis=2).astype(jnp.bfloat16)
    grad_down = jnp.sum(down_recv.astype(jnp.float32), axis=2).astype(jnp.bfloat16)
    partial_rows = input_grad.reshape(group_rows, features).astype(jnp.bfloat16)
    pieces = partial_rows.reshape(tensor_count, rows_here, features)
    received = lax.all_to_all(pieces, "tensor", split_axis=0, concat_axis=0, tiled=True)
    grad_in = jnp.sum(received.astype(jnp.float32), axis=0).astype(jnp.bfloat16)
    return (grad_in, grad_up, grad_down)

def solution(mesh):
    gathers = mesh.shape["seq"] == 4 and mesh.shape["tensor"] % 2 == 0
    return jax.shard_map(
        local_all_tokens if gathers else local,
        mesh=mesh,
        in_specs=(
            P(("seq", "tensor"), None),
            P(("seq", "tensor"), None),
            P("tensor", None, None, None),
            P("tensor", None),
            P("tensor", None, None, None),
            P("tensor", None),
        ),
        out_specs=(
            P(("seq", "tensor"), None),
            P("tensor", None, "seq", None),
            P("tensor", None, "seq", None),
        ),
        check_vma=False,
    )
```

```python
import functools
import math

import jax
import jax.numpy as jnp
from jax import lax
from jax.experimental import pallas as pl
from jax.experimental.pallas import tpu as pltpu
from jax.sharding import PartitionSpec as P

MESH = pl.DeviceIdType.MESH
MIB = 1024 * 1024


def gather_kernel(
    zs, in_ref, go_ref, out, loc, own_send, own_recv, recv, zsend, xysend, hsend, sib_send, sib_recv
):
    s, t = lax.axis_index("seq"), lax.axis_index("tensor")
    z, c = t // 2, t % 2
    x, y = s % 2, s // 2
    xn, yn, dg = y * 2 + (1 - x), (1 - y) * 2 + x, (1 - y) * 2 + (1 - x)
    sib = z * 2 + (1 - c)

    barrier = pltpu.get_barrier_semaphore()
    for dev in ((s, sib), (xn, t), (yn, t)):
        pl.semaphore_signal(barrier, inc=1, device_id=dev, device_id_type=MESH)

    @pl.when(z < zs - 1)
    def _():
        pl.semaphore_signal(barrier, inc=1, device_id=(s, t + 2), device_id_type=MESH)

    @pl.when(z > 0)
    def _():
        pl.semaphore_signal(barrier, inc=1, device_id=(s, t - 2), device_id_type=MESH)

    pl.semaphore_wait(barrier, 3 + jnp.minimum(z, 1) + jnp.minimum(zs - 1 - z, 1))

    def copy(ref, send, recv_sem, dev):
        return pltpu.make_async_remote_copy(
            src_ref=ref, dst_ref=ref, send_sem=send, recv_sem=recv_sem, device_id=dev, device_id_type=MESH
        )

    def own_copy(a, ref):
        return pltpu.make_async_remote_copy(
            src_ref=ref,
            dst_ref=out.at[a, s, z, c],
            send_sem=own_send.at[a],
            recv_sem=own_recv.at[a],
            device_id=(s, sib),
            device_id_type=MESH,
        )

    def unit(q, o):
        return out.at[c, q, o]

    def right(o):
        return copy(unit(s, o), zsend.at[0, o], recv.at[s, o, 0], (s, t + 2))

    def left(o):
        return copy(unit(s, o), zsend.at[1, o], recv.at[s, o, 0], (s, t - 2))

    def to_x(o):
        return copy(unit(s, o), xysend.at[0, o], recv.at[s, o, 0], (xn, t))

    def to_y(o):
        return copy(unit(s, o), xysend.at[1, o], recv.at[s, o, 0], (yn, t))

    def half_y(o):
        return copy(out.at[c, xn, o, 0], hsend.at[0, o], recv.at[xn, o, 0], (yn, t))

    def half_x(o):
        return copy(out.at[c, yn, o, 1], hsend.at[1, o], recv.at[yn, o, 1], (xn, t))

    def to_sib(q, o):
        return copy(unit(q, o), sib_send.at[q, o], sib_recv.at[q, o], (s, sib))

    def from_sib(q, o):
        return copy(out.at[1 - c, q, o], sib_send.at[q, o], sib_recv.at[q, o], (s, sib))

    def got(q, o):
        copy(unit(q, o), xysend.at[0, o], recv.at[q, o, 0], (xn, t)).wait_recv()

    def got_half(o, h):
        copy(out.at[c, dg, o, h], hsend.at[h, o], recv.at[dg, o, h], (xn, t)).wait_recv()

    def spread(o):
        to_x(o).start()
        to_y(o).start()

    def from_xy(o):
        got(xn, o)
        half_y(o).start()
        to_sib(xn, o).start()
        got(yn, o)
        half_x(o).start()
        to_sib(yn, o).start()

    def from_diagonal(o):
        got_half(o, 0)
        got_half(o, 1)
        to_sib(dg, o).start()

    def at_distance(d, act):
        if d == 0:
            act(z)
            return
        pl.when(z - d >= 0)(lambda: act(z - d))
        pl.when(z + d < zs)(lambda: act(z + d))

    locals_ = [
        pltpu.make_async_copy(ref, out.at[a, s, z, c], loc.at[a]) for a, ref in enumerate((in_ref, go_ref))
    ]
    owns = [own_copy(a, ref) for a, ref in enumerate((in_ref, go_ref))]
    for one in owns + locals_:
        one.start()
    for one in locals_:
        one.wait()
    for one in owns:
        one.wait_recv()

    pl.when(z < zs - 1)(lambda: right(z).start())
    pl.when(z > 0)(lambda: left(z).start())
    spread(z)
    for d in range(1, zs):

        @pl.when(z - d >= 0)
        def _(d=d):
            o = z - d
            got(s, o)
            pl.when(z < zs - 1)(lambda: right(o).start())
            spread(o)
            to_sib(s, o).start()

        @pl.when(z + d < zs)
        def _(d=d):
            o = z + d
            got(s, o)
            pl.when(z > 0)(lambda: left(o).start())
            spread(o)
            to_sib(s, o).start()

        at_distance(d - 1, from_xy)
        if d >= 2:
            at_distance(d - 2, from_diagonal)
    at_distance(zs - 1, from_xy)
    if zs >= 2:
        at_distance(zs - 2, from_diagonal)
    at_distance(zs - 1, from_diagonal)

    for one in owns:
        one.wait_send()
    for o in range(zs):
        pl.when((o <= z) & (z < zs - 1))(lambda o=o: right(o).wait_send())
        pl.when((o >= z) & (z > 0))(lambda o=o: left(o).wait_send())
        to_x(o).wait_send()
        to_y(o).wait_send()
        half_y(o).wait_send()
        half_x(o).wait_send()
        for q in (xn, yn, dg):
            to_sib(q, o).wait_send()
            from_sib(q, o).wait_recv()

        @pl.when(z != o)
        def _(o=o):
            to_sib(s, o).wait_send()
            from_sib(s, o).wait_recv()


def gather_all(inputs, grad_out, seqs, zs):
    rows, features = inputs.shape
    dma = pltpu.SemaphoreType.DMA
    return pl.pallas_call(
        functools.partial(gather_kernel, zs),
        out_shape=jax.ShapeDtypeStruct((2, seqs, zs, 2, rows, features), inputs.dtype),
        in_specs=[pl.BlockSpec(memory_space=pl.ANY)] * 2,
        out_specs=pl.BlockSpec(memory_space=pl.ANY),
        scratch_shapes=[
            dma((2,)),
            dma((2,)),
            dma((2,)),
            dma((seqs, zs, 2)),
            dma((2, zs)),
            dma((2, zs)),
            dma((2, zs)),
            dma((seqs, zs)),
            dma((seqs, zs)),
        ],
        compiler_params=pltpu.CompilerParams(collective_id=0, has_side_effects=True),
        name="gather_all",
    )(inputs, grad_out)


def picked_blocks(ref, index, j, slots, width):
    return jnp.concatenate(
        [ref[:, pl.ds(pl.multiple_of(index[j, k] * width, width), width)] for k in range(slots)], axis=1
    )


def forward(xs, gs, up, down):
    slots, width, _ = up.shape
    preact = jnp.dot(xs, up.reshape(slots * width, width), preferred_element_type=jnp.float32)
    down_wide = jnp.concatenate([down[k] for k in range(slots)], axis=1)
    hidden_grad = lax.dot_general(
        gs, down_wide, (((1,), (1,)), ((), ())), preferred_element_type=jnp.float32
    )
    gating = jax.nn.sigmoid(preact)
    pg = (hidden_grad * gating * (1.0 + preact * (1.0 - gating))).astype(jnp.bfloat16)
    return (preact * gating).astype(jnp.bfloat16), pg


def input_kernel(ui, di, pos, x_ref, g_ref, up_ref, down_ref, out_ref, acc):
    j = pl.program_id(0)
    slots, width = up_ref.shape[1], up_ref.shape[2]

    @pl.when(j == 0)
    def _():
        acc[...] = jnp.zeros_like(acc)

    together = up_ref.shape[0]
    terms = []
    for u in range(together):
        row = j * together + u
        xs = picked_blocks(x_ref, ui, row, slots, width)
        gs = picked_blocks(g_ref, di, row, slots, width)
        up = up_ref[u]
        _, pg = forward(xs, gs, up, down_ref[u])
        terms.append(
            lax.dot_general(
                pg,
                up.reshape(slots * width, width),
                (((1,), (1,)), ((), ())),
                preferred_element_type=jnp.float32,
            )
        )
    for u in range(together):
        for k in range(slots):
            where = pl.ds(pl.multiple_of(ui[j * together + u, k] * width, width), width)
            acc[:, where] += terms[u][:, k * width : (k + 1) * width]

    @pl.when(j == pl.num_programs(0) - 1)
    def _():
        out_ref[...] = acc[...].astype(out_ref.dtype)


def input_part(up_index, down_index, pos, both, up_blocks, down_blocks, rows):
    count, slots, width, _ = up_blocks.shape
    features = both.shape[2]
    together = math.gcd(count, 4)
    weight = pl.BlockSpec((together, slots, width, width), lambda j, *_: (j, 0, 0, 0))
    return pl.pallas_call(
        input_kernel,
        out_shape=jax.ShapeDtypeStruct((rows, features), both.dtype),
        grid_spec=pltpu.PrefetchScalarGridSpec(
            num_scalar_prefetch=3,
            grid=(count // together,),
            in_specs=[
                pl.BlockSpec(
                    (None, rows, features), lambda j, ui, di, pos: (0, pos[0], 0), pipeline_mode=pl.Buffered(1)
                ),
                pl.BlockSpec(
                    (None, rows, features), lambda j, ui, di, pos: (1, pos[0], 0), pipeline_mode=pl.Buffered(1)
                ),
                weight,
                weight,
            ],
            out_specs=pl.BlockSpec((rows, features), lambda j, *_: (0, 0), pipeline_mode=pl.Buffered(1)),
            scratch_shapes=[pltpu.VMEM((rows, features), jnp.float32)],
        ),
        compiler_params=pltpu.CompilerParams(vmem_limit_bytes=40 * MIB),
        cost_estimate=pl.CostEstimate(
            flops=6 * rows * count * slots * width * width,
            bytes_accessed=4 * count * slots * width * width + 6 * rows * features,
            transcendentals=rows * count * width,
        ),
        name="input_part",
    )(up_index, down_index, pos, both, both, up_blocks, down_blocks)


def grads_kernel(factor, ui, di, pos, x_ref, g_ref, up_ref, down_ref, gup_ref, gdown_ref, xq, turned):
    j = pl.program_id(0)
    slots, width = up_ref.shape[1], up_ref.shape[2]
    share = gup_ref.shape[2]
    mine = pl.ds(pl.multiple_of(pos[0] * share, share), share)

    @pl.when(j == 0)
    def _():
        def one(b, carry):
            for u in range(turned.shape[0]):
                block = b * turned.shape[0] + u
                turned[u] = x_ref[:, pl.ds(pl.multiple_of(block * width, width), width)].T
                xq[block] = turned[u, mine, :]
            return carry

        lax.fori_loop(0, xq.shape[0] // turned.shape[0], one, 0)

    together = up_ref.shape[0]
    for u in range(together):
        row = j * together + u
        xs = picked_blocks(x_ref, ui, row, slots, width)
        gs = picked_blocks(g_ref, di, row, slots, width)
        activated, pg = forward(xs, gs, up_ref[u], down_ref[u])
        quarter = jnp.concatenate([xq[ui[row, k]] for k in range(slots)], axis=0)
        gup = jnp.dot(quarter, pg, preferred_element_type=jnp.float32) * factor
        gup_ref[u] = gup.astype(gup_ref.dtype).reshape(slots, share, width)
        turned[u] = activated.T
        gdown = jnp.dot(turned[u, mine, :], gs, preferred_element_type=jnp.float32) * factor
        for k in range(slots):
            gdown_ref[u, k] = gdown[:, k * width : (k + 1) * width].astype(gdown_ref.dtype)


def block_grads(up_index, down_index, pos, both, up_blocks, down_blocks, share, factor):
    count, slots, width, _ = up_blocks.shape
    _, tokens, features = both.shape
    together = math.gcd(count, 2)
    weight = pl.BlockSpec((together, slots, width, width), lambda j, *_: (j, 0, 0, 0))
    result = pl.BlockSpec((together, slots, share, width), lambda j, *_: (j, 0, 0, 0))
    shape = jax.ShapeDtypeStruct((count, slots, share, width), both.dtype)
    return pl.pallas_call(
        functools.partial(grads_kernel, factor),
        out_shape=[shape, shape],
        grid_spec=pltpu.PrefetchScalarGridSpec(
            num_scalar_prefetch=3,
            grid=(count // together,),
            in_specs=[
                pl.BlockSpec((None, tokens, features), lambda j, *_: (0, 0, 0), pipeline_mode=pl.Buffered(1)),
                pl.BlockSpec((None, tokens, features), lambda j, *_: (1, 0, 0), pipeline_mode=pl.Buffered(1)),
                weight,
                weight,
            ],
            out_specs=[result, result],
            scratch_shapes=[
                pltpu.VMEM((features // width, share, tokens), both.dtype),
                pltpu.VMEM((together, width, tokens), both.dtype),
            ],
        ),
        compiler_params=pltpu.CompilerParams(vmem_limit_bytes=56 * MIB),
        cost_estimate=pl.CostEstimate(
            flops=6 * tokens * count * slots * width * width,
            bytes_accessed=6 * count * slots * width * width + 4 * tokens * features,
            transcendentals=tokens * count * width,
        ),
        name="block_grads",
    )(up_index, down_index, pos, both, both, up_blocks, down_blocks)


def local_all_tokens(inputs, grad_out, up_blocks, up_index, down_blocks, down_index):
    tensor_count = lax.axis_size("tensor")
    seq_count = lax.axis_size("seq")
    rows_here, features = inputs.shape
    block = up_blocks.shape[2]
    group_rows = rows_here * tensor_count
    factor = 1.0 / math.sqrt(group_rows * seq_count)
    both = gather_all(inputs, grad_out, seq_count, tensor_count // 2)
    both = both.reshape(2, group_rows * seq_count, features)
    pos = lax.axis_index("seq").astype(jnp.int32).reshape(1)
    part = input_part(up_index, down_index, pos, both, up_blocks, down_blocks, group_rows)
    pieces = part.reshape(tensor_count, rows_here, features)
    received = lax.all_to_all(pieces, "tensor", split_axis=0, concat_axis=0, tiled=True)
    grad_up, grad_down = block_grads(
        up_index, down_index, pos, both, up_blocks, down_blocks, block // seq_count, factor
    )
    grad_in = jnp.sum(received.astype(jnp.float32), axis=0).astype(jnp.bfloat16)
    return (grad_in, grad_up, grad_down)


def local(inputs, grad_out, up_blocks, up_index, down_blocks, down_index):
    tensor_count = lax.axis_size("tensor")
    seq_count = lax.axis_size("seq")
    rows_here, features = inputs.shape
    local_blocks, slots, block, _ = up_blocks.shape
    blocks_wide = features // block
    group_rows = rows_here * tensor_count
    factor = 1.0 / math.sqrt(group_rows * seq_count)
    flat_index = up_index.reshape(-1)
    in_rows = lax.all_gather(inputs, "tensor", axis=0, tiled=True)
    grad_rows = lax.all_gather(grad_out, "tensor", axis=0, tiled=True)
    piece_rows = in_rows.shape[0]
    picked = jnp.take(in_rows.reshape(piece_rows, blocks_wide, block), up_index, axis=1)
    picked_grad = jnp.take(grad_rows.reshape(piece_rows, blocks_wide, block), down_index, axis=1)
    preact = jnp.einsum("rjkc,jkch->rjh", picked, up_blocks, preferred_element_type=jnp.float32)
    hidden_grad = jnp.einsum(
        "rjko,jkho->rjh", picked_grad, down_blocks, preferred_element_type=jnp.float32
    )
    gating = jax.nn.sigmoid(preact)
    activated = (preact * gating).astype(jnp.bfloat16)
    preact_grad = (hidden_grad * gating * (1.0 + preact * (1.0 - gating))).astype(jnp.bfloat16)
    up_sum = jnp.einsum("rjkc,rjh->jkch", picked, preact_grad, preferred_element_type=jnp.float32)
    down_sum = jnp.einsum(
        "rjh,rjko->jkho", activated, picked_grad, preferred_element_type=jnp.float32
    )
    contrib = jnp.einsum(
        "rjh,jkch->rjkc", preact_grad, up_blocks, preferred_element_type=jnp.float32
    )
    contrib = contrib.reshape(piece_rows, local_blocks * slots, block)
    partial_value = (
        jnp.zeros((piece_rows, blocks_wide, block), jnp.float32).at[:, flat_index].add(contrib)
    )
    input_grad = partial_value
    up_sum, down_sum, input_grad = (up_sum, down_sum, input_grad)
    share = block // seq_count
    up_part = (
        (up_sum * factor).astype(jnp.bfloat16).reshape(local_blocks, slots, seq_count, share, block)
    )
    down_part = (
        (down_sum * factor)
        .astype(jnp.bfloat16)
        .reshape(local_blocks, slots, seq_count, share, block)
    )
    up_recv, down_recv = (
        lax.all_to_all(up_part, "seq", split_axis=2, concat_axis=2, tiled=True),
        lax.all_to_all(down_part, "seq", split_axis=2, concat_axis=2, tiled=True),
    )
    grad_up = jnp.sum(up_recv.astype(jnp.float32), axis=2).astype(jnp.bfloat16)
    grad_down = jnp.sum(down_recv.astype(jnp.float32), axis=2).astype(jnp.bfloat16)
    partial_rows = input_grad.reshape(group_rows, features).astype(jnp.bfloat16)
    pieces = partial_rows.reshape(tensor_count, rows_here, features)
    received = lax.all_to_all(pieces, "tensor", split_axis=0, concat_axis=0, tiled=True)
    grad_in = jnp.sum(received.astype(jnp.float32), axis=0).astype(jnp.bfloat16)
    return (grad_in, grad_up, grad_down)

def solution(mesh):
    gathers = mesh.shape["seq"] == 4 and mesh.shape["tensor"] % 2 == 0
    return jax.shard_map(
        local_all_tokens if gathers else local,
        mesh=mesh,
        in_specs=(
            P(("seq", "tensor"), None),
            P(("seq", "tensor"), None),
            P("tensor", None, None, None),
            P("tensor", None),
            P("tensor", None, None, None),
            P("tensor", None),
        ),
        out_specs=(
            P(("seq", "tensor"), None),
            P("tensor", None, "seq", None),
            P("tensor", None, "seq", None),
        ),
        check_vma=False,
    )
```

```python
import functools
import math

import jax
import jax.numpy as jnp
from jax import lax
from jax.experimental import pallas as pl
from jax.experimental.pallas import tpu as pltpu
from jax.sharding import PartitionSpec as P

MESH = pl.DeviceIdType.MESH
MIB = 1024 * 1024


def place():
    s, t = lax.axis_index("seq"), lax.axis_index("tensor")
    z, c = t // 2, t % 2
    x, y = s % 2, s // 2
    xn, yn = y * 2 + (1 - x), (1 - y) * 2 + x
    return s, t, z, c, (xn, t), (yn, t), (s, z * 2 + (1 - c))


def remote(src, dst, send, recv, dev):
    return pltpu.make_async_remote_copy(
        src_ref=src, dst_ref=dst, send_sem=send, recv_sem=recv, device_id=dev, device_id_type=MESH
    )


def gather_kernel(
    zs, in_ref, go_ref, out, loc, own_send, own_recv, zrecv, zsend, recv, send, sib_send, sib_recv
):
    s, t, z, c, xdev, ydev, sib = place()
    r = z % 2
    mate = z + 1 - 2 * r

    barrier = pltpu.get_barrier_semaphore()
    for dev in (sib, xdev, ydev):
        pl.semaphore_signal(barrier, inc=1, device_id=dev, device_id_type=MESH)

    @pl.when(z < zs - 1)
    def _():
        pl.semaphore_signal(barrier, inc=1, device_id=(s, t + 2), device_id_type=MESH)

    @pl.when(z > 0)
    def _():
        pl.semaphore_signal(barrier, inc=1, device_id=(s, t - 2), device_id_type=MESH)

    pl.semaphore_wait(barrier, 3 + jnp.minimum(z, 1) + jnp.minimum(zs - 1 - z, 1))

    def unit(i):
        return out.at[c, i]

    def right(o):
        return remote(unit(o), unit(o), zsend.at[0, o], zrecv.at[o], (s, t + 2))

    def left(o):
        return remote(unit(o), unit(o), zsend.at[1, o], zrecv.at[o], (s, t - 2))

    def to_x(o, i):
        return remote(unit(o), unit(zs + i), send.at[0, i], recv.at[0, i], xdev)

    def to_y(o, i):
        return remote(unit(o), unit(zs + 2 + i), send.at[1, i], recv.at[1, i], ydev)

    def onward_y():
        return remote(unit(zs), unit(zs + 4), send.at[2, 0], recv.at[2, 0], ydev)

    def onward_x():
        return remote(unit(zs + 3), unit(zs + 5), send.at[2, 1], recv.at[2, 1], xdev)

    def to_sib(i):
        return remote(unit(i), unit(i), sib_send.at[i], sib_recv.at[i], sib)

    def from_sib(i):
        return remote(out.at[1 - c, i], out.at[1 - c, i], sib_send.at[i], sib_recv.at[i], sib)

    shards = list(enumerate((in_ref, go_ref)))
    locals_ = [pltpu.make_async_copy(ref, out.at[a, z, c], loc.at[a]) for a, ref in shards]
    owns = [remote(ref, out.at[a, z, c], own_send.at[a], own_recv.at[a], sib) for a, ref in shards]
    for one in owns + locals_:
        one.start()
    for one in locals_:
        one.wait()
    for one in owns:
        one.wait_recv()

    def from_z(d, o, onward, near):
        right(o).wait_recv()
        if onward is not None:
            onward(o)
        if d == 1:

            @pl.when(near)
            def _():
                to_x(o, 1 - r).start()
                to_y(o, 1 - r).start()

        to_sib(o).start()

    def from_xy(i):
        to_x(z, i).wait_recv()
        pl.when(i == 0)(lambda: onward_y().start())
        to_sib(zs + i).start()
        to_y(z, i).wait_recv()
        pl.when(i == 1)(lambda: onward_x().start())
        to_sib(zs + 2 + i).start()

    pl.when(z < zs - 1)(lambda: right(z).start())
    pl.when(z > 0)(lambda: left(z).start())
    to_x(z, r).start()
    to_y(z, r).start()
    for d in range(1, zs):

        @pl.when(z - d >= 0)
        def _(d=d):
            def on(o):
                pl.when(z < zs - 1)(lambda: right(o).start())

            from_z(d, z - d, on, r == 1)

        @pl.when(z + d < zs)
        def _(d=d):
            def on(o):
                pl.when(z > 0)(lambda: left(o).start())

            from_z(d, z + d, on, r == 0)

        if d == 1:
            from_xy(r)
        if d == 2:
            from_xy(1 - r)
    onward_y().wait_recv()
    to_sib(zs + 4).start()
    onward_x().wait_recv()
    to_sib(zs + 5).start()

    for one in owns:
        one.wait_send()
    for o in range(zs):
        pl.when((o <= z) & (z < zs - 1))(lambda o=o: right(o).wait_send())
        pl.when((o >= z) & (z > 0))(lambda o=o: left(o).wait_send())

        @pl.when(z != o)
        def _(o=o):
            to_sib(o).wait_send()
            from_sib(o).wait_recv()

    for i in range(2):
        to_x(z, i).wait_send()
        to_y(z, i).wait_send()
    onward_y().wait_send()
    onward_x().wait_send()
    for i in range(zs, zs + 6):
        to_sib(i).wait_send()
        from_sib(i).wait_recv()


def gather_first(inputs, grad_out, zs):
    rows, features = inputs.shape
    dma = pltpu.SemaphoreType.DMA
    units = zs + 6
    return pl.pallas_call(
        functools.partial(gather_kernel, zs),
        out_shape=jax.ShapeDtypeStruct((2, units, 2, rows, features), inputs.dtype),
        in_specs=[pl.BlockSpec(memory_space=pl.ANY)] * 2,
        out_specs=pl.BlockSpec(memory_space=pl.ANY),
        scratch_shapes=[
            dma((2,)),
            dma((2,)),
            dma((2,)),
            dma((zs,)),
            dma((2, zs)),
            dma((3, 2)),
            dma((3, 2)),
            dma((units,)),
            dma((units,)),
        ],
        compiler_params=pltpu.CompilerParams(collective_id=0, has_side_effects=True),
        name="gather_first",
    )(inputs, grad_out)


def picked_blocks(ref, index, j, slots, width):
    return jnp.concatenate(
        [ref[:, pl.ds(pl.multiple_of(index[j, k] * width, width), width)] for k in range(slots)], axis=1
    )


def forward(xs, gs, up, down):
    slots, width, _ = up.shape
    preact = jnp.dot(xs, up.reshape(slots * width, width), preferred_element_type=jnp.float32)
    down_wide = jnp.concatenate([down[k] for k in range(slots)], axis=1)
    hidden_grad = lax.dot_general(
        gs, down_wide, (((1,), (1,)), ((), ())), preferred_element_type=jnp.float32
    )
    gating = jax.nn.sigmoid(preact)
    pg = (hidden_grad * gating * (1.0 + preact * (1.0 - gating))).astype(jnp.bfloat16)
    return (preact * gating).astype(jnp.bfloat16), pg


def input_kernel(ui, di, pos, x_ref, g_ref, up_ref, down_ref, out_ref, acc):
    j = pl.program_id(0)
    slots, width = up_ref.shape[1], up_ref.shape[2]

    @pl.when(j == 0)
    def _():
        acc[...] = jnp.zeros_like(acc)

    together = up_ref.shape[0]
    terms = []
    for u in range(together):
        row = j * together + u
        xs = picked_blocks(x_ref, ui, row, slots, width)
        gs = picked_blocks(g_ref, di, row, slots, width)
        up = up_ref[u]
        _, pg = forward(xs, gs, up, down_ref[u])
        terms.append(
            lax.dot_general(
                pg,
                up.reshape(slots * width, width),
                (((1,), (1,)), ((), ())),
                preferred_element_type=jnp.float32,
            )
        )
    for u in range(together):
        for k in range(slots):
            where = pl.ds(pl.multiple_of(ui[j * together + u, k] * width, width), width)
            acc[:, where] += terms[u][:, k * width : (k + 1) * width]

    @pl.when(j == pl.num_programs(0) - 1)
    def _():
        out_ref[...] = acc[...].astype(out_ref.dtype)


def input_part(up_index, down_index, pos, both, up_blocks, down_blocks, rows):
    count, slots, width, _ = up_blocks.shape
    features = both.shape[2]
    together = math.gcd(count, 4)
    weight = pl.BlockSpec((together, slots, width, width), lambda j, *_: (j, 0, 0, 0))
    return pl.pallas_call(
        input_kernel,
        out_shape=jax.ShapeDtypeStruct((rows, features), both.dtype),
        grid_spec=pltpu.PrefetchScalarGridSpec(
            num_scalar_prefetch=3,
            grid=(count // together,),
            in_specs=[
                pl.BlockSpec(
                    (None, rows, features), lambda j, *_: (0, 0, 0), pipeline_mode=pl.Buffered(1)
                ),
                pl.BlockSpec(
                    (None, rows, features), lambda j, *_: (1, 0, 0), pipeline_mode=pl.Buffered(1)
                ),
                weight,
                weight,
            ],
            out_specs=pl.BlockSpec((rows, features), lambda j, *_: (0, 0), pipeline_mode=pl.Buffered(1)),
            scratch_shapes=[pltpu.VMEM((rows, features), jnp.float32)],
        ),
        compiler_params=pltpu.CompilerParams(vmem_limit_bytes=40 * MIB),
        cost_estimate=pl.CostEstimate(
            flops=6 * rows * count * slots * width * width,
            bytes_accessed=4 * count * slots * width * width + 6 * rows * features,
            transcendentals=rows * count * width,
        ),
        name="input_part",
    )(up_index, down_index, pos, both, both, up_blocks, down_blocks)


def grads_kernel(
    factor, rows, first, ui, di, have, up_hbm, down_hbm, gup_ref, gdown_ref, far,
    near_x, near_g, far_x, far_g, up, down, gup_acc, gdown_acc, near_xq, far_xq, near_turned, far_turned,
    fill, near_fill, far_fill, send, recv, sib_send, sib_recv,
):
    s, t, z, c, xdev, ydev, sib = place()
    count, slots, width, _ = up.shape
    share = gup_ref.shape[2]
    mine = pl.ds(pl.multiple_of(s * share, share), share)

    barrier = pltpu.get_barrier_semaphore()
    for dev in (sib, xdev, ydev):
        pl.semaphore_signal(barrier, inc=1, device_id=dev, device_id_type=MESH)
    pl.semaphore_wait(barrier, 3)

    def piece(i):
        return far.at[c, pl.ds(i * rows, rows)]

    def held(i):
        return have.at[c, pl.ds(pl.multiple_of((2 * (1 - z // 2) + i) * rows, rows), rows)]

    def to_x(i):
        return remote(held(i), piece(i), send.at[i], recv.at[i], xdev)

    def to_y(i):
        return remote(held(i), piece(2 + i), send.at[2 + i], recv.at[2 + i], ydev)

    def onward_y():
        return remote(piece(0), piece(4), send.at[4], recv.at[4], ydev)

    def onward_x():
        return remote(piece(3), piece(5), send.at[5], recv.at[5], xdev)

    def to_sib(i):
        return remote(piece(i), piece(i), sib_send.at[i], sib_recv.at[i], sib)

    def from_sib(i):
        other = far.at[1 - c, pl.ds(i * rows, rows)]
        return remote(other, other, sib_send.at[i], sib_recv.at[i], sib)

    sends = (to_x(0), to_x(1), to_y(0), to_y(1), onward_y(), onward_x())
    for i in (0, 3, 1, 2):
        sends[i].start()
    fills = [
        pltpu.make_async_copy(src, dst, fill.at[i])
        for i, (src, dst) in enumerate(((up_hbm, up), (down_hbm, down)))
    ]

    def columns(src, a, dst, sems, b):
        where = pl.ds(pl.multiple_of(b * width, width), width)
        return pltpu.make_async_copy(src.at[a, :, where], dst.at[b], sems.at[a, b])

    def start_columns(src, x, g, sems):
        def one(b, carry):
            columns(src, 0, x, sems, b).start()
            columns(src, 1, g, sems, b).start()
            return carry

        lax.fori_loop(0, x.shape[0], one, 0)

    def wait_columns(src, x, g, sems):
        def one(b, carry):
            columns(src, 0, x, sems, b).wait()
            columns(src, 1, g, sems, b).wait()
            return carry

        lax.fori_loop(0, x.shape[0], one, 0)

    start_columns(have, near_x, near_g, near_fill)
    for one in fills:
        one.start()

    def arrived(i):
        sends[i].wait_recv()

    def turn(x, xq, turned):
        together = turned.shape[0]

        def one(b, carry):
            for u in range(together):
                block = b * together + u
                turned[u] = x[block].T
                xq[block] = turned[u, mine, :]
            return carry

        lax.fori_loop(0, xq.shape[0] // together, one, 0)

    def add(x, g, xq, turned, start, stop, last):
        together = turned.shape[0]

        def one(j, carry):
            for u in range(together):
                row = j * together + u
                xs = jnp.concatenate([x[ui[row, k]] for k in range(slots)], axis=1)
                gs = jnp.concatenate([g[di[row, k]] for k in range(slots)], axis=1)
                activated, pg = forward(xs, gs, up[row], down[row])
                quarter = jnp.concatenate([xq[ui[row, k]] for k in range(slots)], axis=0)
                gup = jnp.dot(quarter, pg, preferred_element_type=jnp.float32)
                gup = gup.reshape(slots, share, width)
                turned[u] = activated.T
                gdown = jnp.dot(turned[u, mine, :], gs, preferred_element_type=jnp.float32)
                if last:
                    gup_ref[row] = ((gup_acc[row] + gup) * factor).astype(gup_ref.dtype)
                else:
                    gup_acc[row] = gup
                for k in range(slots):
                    part = gdown[:, k * width : (k + 1) * width]
                    if last:
                        gdown_ref[row, k] = ((gdown_acc[row, k] + part) * factor).astype(gdown_ref.dtype)
                    else:
                        gdown_acc[row, k] = part
            return carry

        lax.fori_loop(start // together, stop // together, one, 0)

    wait_columns(have, near_x, near_g, near_fill)
    turn(near_x, near_xq, near_turned)
    for one in fills:
        one.wait()
    add(near_x, near_g, near_xq, near_turned, 0, first, False)
    arrived(0)
    sends[4].start()
    to_sib(0).start()
    arrived(3)
    sends[5].start()
    to_sib(3).start()
    add(near_x, near_g, near_xq, near_turned, first, count, False)
    for i in (1, 2, 4, 5):
        arrived(i)
        to_sib(i).start()
    for i in range(6):
        from_sib(i).wait_recv()
    start_columns(far, far_x, far_g, far_fill)
    wait_columns(far, far_x, far_g, far_fill)
    turn(far_x, far_xq, far_turned)
    add(far_x, far_g, far_xq, far_turned, 0, count, True)
    for i in range(6):
        sends[i].wait_send()
        to_sib(i).wait_send()


def block_grads(up_index, down_index, have, up_blocks, down_blocks, rows, share, factor):
    count, slots, width, _ = up_blocks.shape
    _, tokens, features = have.shape
    dtype = have.dtype
    together = math.gcd(count, 2)
    first = count // 2 // together * together
    blocks = features // width
    shape = jax.ShapeDtypeStruct((count, slots, share, width), dtype)
    dma = pltpu.SemaphoreType.DMA
    vmem = pltpu.VMEM
    return pl.pallas_call(
        functools.partial(grads_kernel, factor, rows, first),
        out_shape=[shape, shape, jax.ShapeDtypeStruct((2, 6 * rows, features), dtype)],
        in_specs=[pl.BlockSpec(memory_space=pltpu.SMEM)] * 2 + [pl.BlockSpec(memory_space=pl.ANY)] * 3,
        out_specs=[pl.BlockSpec(memory_space=vmem)] * 2 + [pl.BlockSpec(memory_space=pl.ANY)],
        scratch_shapes=[
            vmem((blocks, tokens, width), dtype),
            vmem((blocks, tokens, width), dtype),
            vmem((blocks, 6 * rows, width), dtype),
            vmem((blocks, 6 * rows, width), dtype),
            vmem(up_blocks.shape, dtype),
            vmem(down_blocks.shape, dtype),
            vmem(shape.shape, jnp.float32),
            vmem(shape.shape, jnp.float32),
            vmem((blocks, share, tokens), dtype),
            vmem((blocks, share, 6 * rows), dtype),
            vmem((together, width, tokens), dtype),
            vmem((together, width, 6 * rows), dtype),
            dma((2,)),
            dma((2, blocks)),
            dma((2, blocks)),
            dma((6,)),
            dma((6,)),
            dma((6,)),
            dma((6,)),
        ],
        compiler_params=pltpu.CompilerParams(
            collective_id=1, has_side_effects=True, vmem_limit_bytes=61 * MIB
        ),
        cost_estimate=pl.CostEstimate(
            flops=10 * tokens * count * slots * width * width,
            bytes_accessed=6 * count * slots * width * width + 6 * tokens * features,
            transcendentals=2 * tokens * count * width,
        ),
        name="block_grads",
    )(up_index, down_index, have, up_blocks, down_blocks)


def local_all_tokens(inputs, grad_out, up_blocks, up_index, down_blocks, down_index):
    tensor_count = lax.axis_size("tensor")
    seq_count = lax.axis_size("seq")
    rows_here, features = inputs.shape
    block = up_blocks.shape[2]
    group_rows = rows_here * tensor_count
    factor = 1.0 / math.sqrt(group_rows * seq_count)
    have = gather_first(inputs, grad_out, tensor_count // 2)
    have = have.reshape(2, -1, features)
    pos = lax.axis_index("seq").astype(jnp.int32).reshape(1)
    part = input_part(up_index, down_index, pos, have, up_blocks, down_blocks, group_rows)
    pieces = part.reshape(tensor_count, rows_here, features)
    received = lax.all_to_all(pieces, "tensor", split_axis=0, concat_axis=0, tiled=True)
    grad_up, grad_down, _ = block_grads(
        up_index, down_index, have, up_blocks, down_blocks, 2 * rows_here, block // seq_count, factor
    )
    grad_in = jnp.sum(received.astype(jnp.float32), axis=0).astype(jnp.bfloat16)
    return (grad_in, grad_up, grad_down)


def local(inputs, grad_out, up_blocks, up_index, down_blocks, down_index):
    tensor_count = lax.axis_size("tensor")
    seq_count = lax.axis_size("seq")
    rows_here, features = inputs.shape
    local_blocks, slots, block, _ = up_blocks.shape
    blocks_wide = features // block
    group_rows = rows_here * tensor_count
    factor = 1.0 / math.sqrt(group_rows * seq_count)
    flat_index = up_index.reshape(-1)
    in_rows = lax.all_gather(inputs, "tensor", axis=0, tiled=True)
    grad_rows = lax.all_gather(grad_out, "tensor", axis=0, tiled=True)
    piece_rows = in_rows.shape[0]
    picked = jnp.take(in_rows.reshape(piece_rows, blocks_wide, block), up_index, axis=1)
    picked_grad = jnp.take(grad_rows.reshape(piece_rows, blocks_wide, block), down_index, axis=1)
    preact = jnp.einsum("rjkc,jkch->rjh", picked, up_blocks, preferred_element_type=jnp.float32)
    hidden_grad = jnp.einsum(
        "rjko,jkho->rjh", picked_grad, down_blocks, preferred_element_type=jnp.float32
    )
    gating = jax.nn.sigmoid(preact)
    activated = (preact * gating).astype(jnp.bfloat16)
    preact_grad = (hidden_grad * gating * (1.0 + preact * (1.0 - gating))).astype(jnp.bfloat16)
    up_sum = jnp.einsum("rjkc,rjh->jkch", picked, preact_grad, preferred_element_type=jnp.float32)
    down_sum = jnp.einsum(
        "rjh,rjko->jkho", activated, picked_grad, preferred_element_type=jnp.float32
    )
    contrib = jnp.einsum(
        "rjh,jkch->rjkc", preact_grad, up_blocks, preferred_element_type=jnp.float32
    )
    contrib = contrib.reshape(piece_rows, local_blocks * slots, block)
    partial_value = (
        jnp.zeros((piece_rows, blocks_wide, block), jnp.float32).at[:, flat_index].add(contrib)
    )
    input_grad = partial_value
    up_sum, down_sum, input_grad = (up_sum, down_sum, input_grad)
    share = block // seq_count
    up_part = (
        (up_sum * factor).astype(jnp.bfloat16).reshape(local_blocks, slots, seq_count, share, block)
    )
    down_part = (
        (down_sum * factor)
        .astype(jnp.bfloat16)
        .reshape(local_blocks, slots, seq_count, share, block)
    )
    up_recv, down_recv = (
        lax.all_to_all(up_part, "seq", split_axis=2, concat_axis=2, tiled=True),
        lax.all_to_all(down_part, "seq", split_axis=2, concat_axis=2, tiled=True),
    )
    grad_up = jnp.sum(up_recv.astype(jnp.float32), axis=2).astype(jnp.bfloat16)
    grad_down = jnp.sum(down_recv.astype(jnp.float32), axis=2).astype(jnp.bfloat16)
    partial_rows = input_grad.reshape(group_rows, features).astype(jnp.bfloat16)
    pieces = partial_rows.reshape(tensor_count, rows_here, features)
    received = lax.all_to_all(pieces, "tensor", split_axis=0, concat_axis=0, tiled=True)
    grad_in = jnp.sum(received.astype(jnp.float32), axis=0).astype(jnp.bfloat16)
    return (grad_in, grad_up, grad_down)

def solution(mesh):
    gathers = mesh.shape["seq"] == 4 and mesh.shape["tensor"] == 8
    return jax.shard_map(
        local_all_tokens if gathers else local,
        mesh=mesh,
        in_specs=(
            P(("seq", "tensor"), None),
            P(("seq", "tensor"), None),
            P("tensor", None, None, None),
            P("tensor", None),
            P("tensor", None, None, None),
            P("tensor", None),
        ),
        out_specs=(
            P(("seq", "tensor"), None),
            P("tensor", None, "seq", None),
            P("tensor", None, "seq", None),
        ),
        check_vma=False,
    )
```

```python
import functools
import math

import jax
import jax.numpy as jnp
from jax import lax
from jax.experimental import pallas as pl
from jax.experimental.pallas import tpu as pltpu
from jax.sharding import PartitionSpec as P

MESH = pl.DeviceIdType.MESH
MIB = 1024 * 1024


def place():
    s, t = lax.axis_index("seq"), lax.axis_index("tensor")
    z, c = t // 2, t % 2
    x, y = s % 2, s // 2
    xn, yn = y * 2 + (1 - x), (1 - y) * 2 + x
    return s, t, z, c, (xn, t), (yn, t), (s, z * 2 + (1 - c))


def remote(src, dst, send, recv, dev):
    return pltpu.make_async_remote_copy(
        src_ref=src, dst_ref=dst, send_sem=send, recv_sem=recv, device_id=dev, device_id_type=MESH
    )


def gather_kernel(
    zs, in_ref, go_ref, out, loc, own_send, own_recv, zrecv, zsend, recv, send, sib_send, sib_recv
):
    s, t, z, c, xdev, ydev, sib = place()
    r = z % 2
    mate = z + 1 - 2 * r

    barrier = pltpu.get_barrier_semaphore()
    for dev in (sib, xdev, ydev):
        pl.semaphore_signal(barrier, inc=1, device_id=dev, device_id_type=MESH)

    @pl.when(z < zs - 1)
    def _():
        pl.semaphore_signal(barrier, inc=1, device_id=(s, t + 2), device_id_type=MESH)

    @pl.when(z > 0)
    def _():
        pl.semaphore_signal(barrier, inc=1, device_id=(s, t - 2), device_id_type=MESH)

    pl.semaphore_wait(barrier, 3 + jnp.minimum(z, 1) + jnp.minimum(zs - 1 - z, 1))

    def unit(i):
        return out.at[c, i]

    def right(o):
        return remote(unit(o), unit(o), zsend.at[0, o], zrecv.at[o], (s, t + 2))

    def left(o):
        return remote(unit(o), unit(o), zsend.at[1, o], zrecv.at[o], (s, t - 2))

    def to_x(o, i):
        return remote(unit(o), unit(zs + i), send.at[0, i], recv.at[0, i], xdev)

    def to_y(o, i):
        return remote(unit(o), unit(zs + 2 + i), send.at[1, i], recv.at[1, i], ydev)

    def onward_y():
        return remote(unit(zs), unit(zs + 4), send.at[2, 0], recv.at[2, 0], ydev)

    def onward_x():
        return remote(unit(zs + 3), unit(zs + 5), send.at[2, 1], recv.at[2, 1], xdev)

    parts = sib_send.shape[1] // 2
    wide = in_ref.shape[1] // parts

    def with_sib(a, i):
        refs = [out.at[a, i, h, :, pl.ds(f * wide, wide)] for h in range(2) for f in range(parts)]
        return [
            remote(ref, ref, sib_send.at[i, n], sib_recv.at[i, n], sib) for n, ref in enumerate(refs)
        ]

    def to_sib(i):
        for one in with_sib(c, i):
            one.start()

    def sent_sib(i):
        for one in with_sib(c, i):
            one.wait_send()

    def from_sib(i):
        for one in with_sib(1 - c, i):
            one.wait_recv()

    shards = list(enumerate((in_ref, go_ref)))
    locals_ = [pltpu.make_async_copy(ref, out.at[a, z, c], loc.at[a]) for a, ref in shards]
    owns = [remote(ref, out.at[a, z, c], own_send.at[a], own_recv.at[a], sib) for a, ref in shards]
    for one in owns + locals_:
        one.start()
    for one in locals_:
        one.wait()
    for one in owns:
        one.wait_recv()

    def from_z(d, o, onward, near):
        right(o).wait_recv()
        if onward is not None:
            onward(o)
        if d == 1:

            @pl.when(near)
            def _():
                to_x(o, 1 - r).start()
                to_y(o, 1 - r).start()

        to_sib(o)

    def from_xy(i):
        to_x(z, i).wait_recv()
        pl.when(i == 0)(lambda: onward_y().start())
        to_sib(zs + i)
        to_y(z, i).wait_recv()
        pl.when(i == 1)(lambda: onward_x().start())
        to_sib(zs + 2 + i)

    pl.when(z < zs - 1)(lambda: right(z).start())
    pl.when(z > 0)(lambda: left(z).start())
    to_x(z, r).start()
    to_y(z, r).start()
    for d in range(1, zs):

        @pl.when(z - d >= 0)
        def _(d=d):
            def on(o):
                pl.when(z < zs - 1)(lambda: right(o).start())

            from_z(d, z - d, on, r == 1)

        @pl.when(z + d < zs)
        def _(d=d):
            def on(o):
                pl.when(z > 0)(lambda: left(o).start())

            from_z(d, z + d, on, r == 0)

        if d == 1:
            from_xy(r)
        if d == 2:
            from_xy(1 - r)
    onward_y().wait_recv()
    to_sib(zs + 4)
    onward_x().wait_recv()
    to_sib(zs + 5)

    for one in owns:
        one.wait_send()
    for o in range(zs):
        pl.when((o <= z) & (z < zs - 1))(lambda o=o: right(o).wait_send())
        pl.when((o >= z) & (z > 0))(lambda o=o: left(o).wait_send())

        @pl.when(z != o)
        def _(o=o):
            sent_sib(o)
            from_sib(o)

    for i in range(2):
        to_x(z, i).wait_send()
        to_y(z, i).wait_send()
    onward_y().wait_send()
    onward_x().wait_send()
    for i in range(zs, zs + 6):
        sent_sib(i)
        from_sib(i)


def gather_first(inputs, grad_out, zs):
    rows, features = inputs.shape
    dma = pltpu.SemaphoreType.DMA
    units = zs + 6
    return pl.pallas_call(
        functools.partial(gather_kernel, zs),
        out_shape=jax.ShapeDtypeStruct((2, units, 2, rows, features), inputs.dtype),
        in_specs=[pl.BlockSpec(memory_space=pl.ANY)] * 2,
        out_specs=pl.BlockSpec(memory_space=pl.ANY),
        scratch_shapes=[
            dma((2,)),
            dma((2,)),
            dma((2,)),
            dma((zs,)),
            dma((2, zs)),
            dma((3, 2)),
            dma((3, 2)),
            dma((units, 4)),
            dma((units, 4)),
        ],
        compiler_params=pltpu.CompilerParams(collective_id=0, has_side_effects=True),
        name="gather_first",
    )(inputs, grad_out)


def picked_blocks(ref, index, j, slots, width):
    return jnp.concatenate(
        [ref[:, pl.ds(pl.multiple_of(index[j, k] * width, width), width)] for k in range(slots)], axis=1
    )


def forward(xs, gs, up, down):
    slots, width, _ = up.shape
    preact = jnp.dot(xs, up.reshape(slots * width, width), preferred_element_type=jnp.float32)
    down_wide = jnp.concatenate([down[k] for k in range(slots)], axis=1)
    hidden_grad = lax.dot_general(
        gs, down_wide, (((1,), (1,)), ((), ())), preferred_element_type=jnp.float32
    )
    gating = jax.nn.sigmoid(preact)
    pg = (hidden_grad * gating * (1.0 + preact * (1.0 - gating))).astype(jnp.bfloat16)
    return (preact * gating).astype(jnp.bfloat16), pg


def input_kernel(ui, di, pos, x_ref, g_ref, up_ref, down_ref, out_ref, acc):
    j = pl.program_id(0)
    slots, width = up_ref.shape[1], up_ref.shape[2]

    @pl.when(j == 0)
    def _():
        acc[...] = jnp.zeros_like(acc)

    together = up_ref.shape[0]
    terms = []
    for u in range(together):
        row = j * together + u
        xs = picked_blocks(x_ref, ui, row, slots, width)
        gs = picked_blocks(g_ref, di, row, slots, width)
        up = up_ref[u]
        _, pg = forward(xs, gs, up, down_ref[u])
        terms.append(
            lax.dot_general(
                pg,
                up.reshape(slots * width, width),
                (((1,), (1,)), ((), ())),
                preferred_element_type=jnp.float32,
            )
        )
    for u in range(together):
        for k in range(slots):
            where = pl.ds(pl.multiple_of(ui[j * together + u, k] * width, width), width)
            acc[:, where] += terms[u][:, k * width : (k + 1) * width]

    @pl.when(j == pl.num_programs(0) - 1)
    def _():
        out_ref[...] = acc[...].astype(out_ref.dtype)


def input_part(up_index, down_index, pos, both, up_blocks, down_blocks, rows):
    count, slots, width, _ = up_blocks.shape
    features = both.shape[2]
    together = math.gcd(count, 4)
    weight = pl.BlockSpec((together, slots, width, width), lambda j, *_: (j, 0, 0, 0))
    return pl.pallas_call(
        input_kernel,
        out_shape=jax.ShapeDtypeStruct((rows, features), both.dtype),
        grid_spec=pltpu.PrefetchScalarGridSpec(
            num_scalar_prefetch=3,
            grid=(count // together,),
            in_specs=[
                pl.BlockSpec(
                    (None, rows, features), lambda j, *_: (0, 0, 0), pipeline_mode=pl.Buffered(1)
                ),
                pl.BlockSpec(
                    (None, rows, features), lambda j, *_: (1, 0, 0), pipeline_mode=pl.Buffered(1)
                ),
                weight,
                weight,
            ],
            out_specs=pl.BlockSpec((rows, features), lambda j, *_: (0, 0), pipeline_mode=pl.Buffered(1)),
            scratch_shapes=[pltpu.VMEM((rows, features), jnp.float32)],
        ),
        compiler_params=pltpu.CompilerParams(vmem_limit_bytes=60 * MIB),
        cost_estimate=pl.CostEstimate(
            flops=6 * rows * count * slots * width * width,
            bytes_accessed=4 * count * slots * width * width + 6 * rows * features,
            transcendentals=rows * count * width,
        ),
        name="input_part",
    )(up_index, down_index, pos, both, both, up_blocks, down_blocks)


def grads_kernel(
    factor, rows, first, ui, di, have, up_hbm, down_hbm, gup_ref, gdown_ref, far,
    near_x, near_g, far_x, far_g, up, down, gup_acc, gdown_acc, near_xq, far_xq, near_turned, far_turned,
    fill, near_fill, far_fill, send, recv, sib_send, sib_recv,
):
    s, t, z, c, xdev, ydev, sib = place()
    count, slots, width, _ = up.shape
    share = gup_ref.shape[2]
    mine = pl.ds(pl.multiple_of(s * share, share), share)

    barrier = pltpu.get_barrier_semaphore()
    for dev in (sib, xdev, ydev):
        pl.semaphore_signal(barrier, inc=1, device_id=dev, device_id_type=MESH)
    pl.semaphore_wait(barrier, 3)

    def piece(i):
        return far.at[c, pl.ds(i * rows, rows)]

    def held(i):
        return have.at[c, pl.ds(pl.multiple_of((2 * (1 - z // 2) + i) * rows, rows), rows)]

    def to_x(i):
        return remote(held(i), piece(i), send.at[i], recv.at[i], xdev)

    def to_y(i):
        return remote(held(i), piece(2 + i), send.at[2 + i], recv.at[2 + i], ydev)

    def onward_y():
        return remote(piece(0), piece(4), send.at[4], recv.at[4], ydev)

    def onward_x():
        return remote(piece(3), piece(5), send.at[5], recv.at[5], xdev)

    def to_sib(i):
        return remote(piece(i), piece(i), sib_send.at[i], sib_recv.at[i], sib)

    def from_sib(i):
        other = far.at[1 - c, pl.ds(i * rows, rows)]
        return remote(other, other, sib_send.at[i], sib_recv.at[i], sib)

    sends = (to_x(0), to_x(1), to_y(0), to_y(1), onward_y(), onward_x())
    for i in (0, 3, 1, 2):
        sends[i].start()
    fills = [
        pltpu.make_async_copy(src, dst, fill.at[i])
        for i, (src, dst) in enumerate(((up_hbm, up), (down_hbm, down)))
    ]

    def columns(src, a, dst, sems, b):
        where = pl.ds(pl.multiple_of(b * width, width), width)
        return pltpu.make_async_copy(src.at[a, :, where], dst.at[b], sems.at[a, b])

    def start_columns(src, x, g, sems):
        def one(b, carry):
            columns(src, 0, x, sems, b).start()
            columns(src, 1, g, sems, b).start()
            return carry

        lax.fori_loop(0, x.shape[0], one, 0)

    def wait_columns(src, x, g, sems):
        def one(b, carry):
            columns(src, 0, x, sems, b).wait()
            columns(src, 1, g, sems, b).wait()
            return carry

        lax.fori_loop(0, x.shape[0], one, 0)

    start_columns(have, near_x, near_g, near_fill)
    for one in fills:
        one.start()

    def arrived(i):
        sends[i].wait_recv()

    def turn(x, xq, turned):
        together = turned.shape[0]

        def one(b, carry):
            for u in range(together):
                block = b * together + u
                turned[u] = x[block].T
                xq[block] = turned[u, mine, :]
            return carry

        lax.fori_loop(0, xq.shape[0] // together, one, 0)

    def add(x, g, xq, turned, start, stop, last):
        together = turned.shape[0]

        def one(j, carry):
            for u in range(together):
                row = j * together + u
                xs = jnp.concatenate([x[ui[row, k]] for k in range(slots)], axis=1)
                gs = jnp.concatenate([g[di[row, k]] for k in range(slots)], axis=1)
                activated, pg = forward(xs, gs, up[row], down[row])
                quarter = jnp.concatenate([xq[ui[row, k]] for k in range(slots)], axis=0)
                gup = jnp.dot(quarter, pg, preferred_element_type=jnp.float32)
                gup = gup.reshape(slots, share, width)
                turned[u] = activated.T
                gdown = jnp.dot(turned[u, mine, :], gs, preferred_element_type=jnp.float32)
                if last:
                    gup_ref[row] = ((gup_acc[row] + gup) * factor).astype(gup_ref.dtype)
                else:
                    gup_acc[row] = gup
                for k in range(slots):
                    part = gdown[:, k * width : (k + 1) * width]
                    if last:
                        gdown_ref[row, k] = ((gdown_acc[row, k] + part) * factor).astype(gdown_ref.dtype)
                    else:
                        gdown_acc[row, k] = part
            return carry

        lax.fori_loop(start // together, stop // together, one, 0)

    wait_columns(have, near_x, near_g, near_fill)
    turn(near_x, near_xq, near_turned)
    for one in fills:
        one.wait()
    add(near_x, near_g, near_xq, near_turned, 0, first, False)
    arrived(0)
    sends[4].start()
    to_sib(0).start()
    arrived(3)
    sends[5].start()
    to_sib(3).start()
    add(near_x, near_g, near_xq, near_turned, first, count, False)
    for i in (1, 2, 4, 5):
        arrived(i)
        to_sib(i).start()
    for i in range(6):
        from_sib(i).wait_recv()
    start_columns(far, far_x, far_g, far_fill)
    wait_columns(far, far_x, far_g, far_fill)
    turn(far_x, far_xq, far_turned)
    add(far_x, far_g, far_xq, far_turned, 0, count, True)
    for i in range(6):
        sends[i].wait_send()
        to_sib(i).wait_send()


def block_grads(up_index, down_index, have, up_blocks, down_blocks, rows, share, factor):
    count, slots, width, _ = up_blocks.shape
    _, tokens, features = have.shape
    dtype = have.dtype
    together = math.gcd(count, 4)
    first = count // 2 // together * together
    blocks = features // width
    shape = jax.ShapeDtypeStruct((count, slots, share, width), dtype)
    dma = pltpu.SemaphoreType.DMA
    vmem = pltpu.VMEM
    return pl.pallas_call(
        functools.partial(grads_kernel, factor, rows, first),
        out_shape=[shape, shape, jax.ShapeDtypeStruct((2, 6 * rows, features), dtype)],
        in_specs=[pl.BlockSpec(memory_space=pltpu.SMEM)] * 2 + [pl.BlockSpec(memory_space=pl.ANY)] * 3,
        out_specs=[pl.BlockSpec(memory_space=vmem)] * 2 + [pl.BlockSpec(memory_space=pl.ANY)],
        scratch_shapes=[
            vmem((blocks, tokens, width), dtype),
            vmem((blocks, tokens, width), dtype),
            vmem((blocks, 6 * rows, width), dtype),
            vmem((blocks, 6 * rows, width), dtype),
            vmem(up_blocks.shape, dtype),
            vmem(down_blocks.shape, dtype),
            vmem(shape.shape, jnp.float32),
            vmem(shape.shape, jnp.float32),
            vmem((blocks, share, tokens), dtype),
            vmem((blocks, share, 6 * rows), dtype),
            vmem((together, width, tokens), dtype),
            vmem((together, width, 6 * rows), dtype),
            dma((2,)),
            dma((2, blocks)),
            dma((2, blocks)),
            dma((6,)),
            dma((6,)),
            dma((6,)),
            dma((6,)),
        ],
        compiler_params=pltpu.CompilerParams(
            collective_id=1, has_side_effects=True, vmem_limit_bytes=61 * MIB
        ),
        cost_estimate=pl.CostEstimate(
            flops=10 * tokens * count * slots * width * width,
            bytes_accessed=6 * count * slots * width * width + 6 * tokens * features,
            transcendentals=2 * tokens * count * width,
        ),
        name="block_grads",
    )(up_index, down_index, have, up_blocks, down_blocks)


def local_all_tokens(inputs, grad_out, up_blocks, up_index, down_blocks, down_index):
    tensor_count = lax.axis_size("tensor")
    seq_count = lax.axis_size("seq")
    rows_here, features = inputs.shape
    block = up_blocks.shape[2]
    group_rows = rows_here * tensor_count
    factor = 1.0 / math.sqrt(group_rows * seq_count)
    have = gather_first(inputs, grad_out, tensor_count // 2)
    have = have.reshape(2, -1, features)
    pos = lax.axis_index("seq").astype(jnp.int32).reshape(1)
    part = input_part(up_index, down_index, pos, have, up_blocks, down_blocks, group_rows)
    pieces = part.reshape(tensor_count, rows_here, features)
    received = lax.all_to_all(pieces, "tensor", split_axis=0, concat_axis=0, tiled=True)
    grad_up, grad_down, _ = block_grads(
        up_index, down_index, have, up_blocks, down_blocks, 2 * rows_here, block // seq_count, factor
    )
    grad_in = jnp.sum(received.astype(jnp.float32), axis=0).astype(jnp.bfloat16)
    return (grad_in, grad_up, grad_down)


def local(inputs, grad_out, up_blocks, up_index, down_blocks, down_index):
    tensor_count = lax.axis_size("tensor")
    seq_count = lax.axis_size("seq")
    rows_here, features = inputs.shape
    local_blocks, slots, block, _ = up_blocks.shape
    blocks_wide = features // block
    group_rows = rows_here * tensor_count
    factor = 1.0 / math.sqrt(group_rows * seq_count)
    flat_index = up_index.reshape(-1)
    in_rows = lax.all_gather(inputs, "tensor", axis=0, tiled=True)
    grad_rows = lax.all_gather(grad_out, "tensor", axis=0, tiled=True)
    piece_rows = in_rows.shape[0]
    picked = jnp.take(in_rows.reshape(piece_rows, blocks_wide, block), up_index, axis=1)
    picked_grad = jnp.take(grad_rows.reshape(piece_rows, blocks_wide, block), down_index, axis=1)
    preact = jnp.einsum("rjkc,jkch->rjh", picked, up_blocks, preferred_element_type=jnp.float32)
    hidden_grad = jnp.einsum(
        "rjko,jkho->rjh", picked_grad, down_blocks, preferred_element_type=jnp.float32
    )
    gating = jax.nn.sigmoid(preact)
    activated = (preact * gating).astype(jnp.bfloat16)
    preact_grad = (hidden_grad * gating * (1.0 + preact * (1.0 - gating))).astype(jnp.bfloat16)
    up_sum = jnp.einsum("rjkc,rjh->jkch", picked, preact_grad, preferred_element_type=jnp.float32)
    down_sum = jnp.einsum(
        "rjh,rjko->jkho", activated, picked_grad, preferred_element_type=jnp.float32
    )
    contrib = jnp.einsum(
        "rjh,jkch->rjkc", preact_grad, up_blocks, preferred_element_type=jnp.float32
    )
    contrib = contrib.reshape(piece_rows, local_blocks * slots, block)
    partial_value = (
        jnp.zeros((piece_rows, blocks_wide, block), jnp.float32).at[:, flat_index].add(contrib)
    )
    input_grad = partial_value
    up_sum, down_sum, input_grad = (up_sum, down_sum, input_grad)
    share = block // seq_count
    up_part = (
        (up_sum * factor).astype(jnp.bfloat16).reshape(local_blocks, slots, seq_count, share, block)
    )
    down_part = (
        (down_sum * factor)
        .astype(jnp.bfloat16)
        .reshape(local_blocks, slots, seq_count, share, block)
    )
    up_recv, down_recv = (
        lax.all_to_all(up_part, "seq", split_axis=2, concat_axis=2, tiled=True),
        lax.all_to_all(down_part, "seq", split_axis=2, concat_axis=2, tiled=True),
    )
    grad_up = jnp.sum(up_recv.astype(jnp.float32), axis=2).astype(jnp.bfloat16)
    grad_down = jnp.sum(down_recv.astype(jnp.float32), axis=2).astype(jnp.bfloat16)
    partial_rows = input_grad.reshape(group_rows, features).astype(jnp.bfloat16)
    pieces = partial_rows.reshape(tensor_count, rows_here, features)
    received = lax.all_to_all(pieces, "tensor", split_axis=0, concat_axis=0, tiled=True)
    grad_in = jnp.sum(received.astype(jnp.float32), axis=0).astype(jnp.bfloat16)
    return (grad_in, grad_up, grad_down)

def solution(mesh):
    gathers = mesh.shape["seq"] == 4 and mesh.shape["tensor"] == 8
    return jax.shard_map(
        local_all_tokens if gathers else local,
        mesh=mesh,
        in_specs=(
            P(("seq", "tensor"), None),
            P(("seq", "tensor"), None),
            P("tensor", None, None, None),
            P("tensor", None),
            P("tensor", None, None, None),
            P("tensor", None),
        ),
        out_specs=(
            P(("seq", "tensor"), None),
            P("tensor", None, "seq", None),
            P("tensor", None, "seq", None),
        ),
        check_vma=False,
    )
```

```python
import functools
import math

import jax
import jax.numpy as jnp
from jax import lax
from jax.experimental import pallas as pl
from jax.experimental.pallas import tpu as pltpu
from jax.sharding import PartitionSpec as P

MESH = pl.DeviceIdType.MESH
MIB = 1024 * 1024


def place():
    s, t = lax.axis_index("seq"), lax.axis_index("tensor")
    z, c = t // 2, t % 2
    x, y = s % 2, s // 2
    xn, yn = y * 2 + (1 - x), (1 - y) * 2 + x
    return s, t, z, c, (xn, t), (yn, t), (s, z * 2 + (1 - c))


def remote(src, dst, send, recv, dev):
    return pltpu.make_async_remote_copy(
        src_ref=src, dst_ref=dst, send_sem=send, recv_sem=recv, device_id=dev, device_id_type=MESH
    )


def gather_kernel(
    zs, in_ref, go_ref, out, loc, own_send, own_recv, zrecv, zsend, recv, send, sib_send, sib_recv
):
    s, t, z, c, xdev, ydev, sib = place()
    r = z % 2
    mate = z + 1 - 2 * r

    barrier = pltpu.get_barrier_semaphore()
    for dev in (sib, xdev, ydev):
        pl.semaphore_signal(barrier, inc=1, device_id=dev, device_id_type=MESH)

    @pl.when(z < zs - 1)
    def _():
        pl.semaphore_signal(barrier, inc=1, device_id=(s, t + 2), device_id_type=MESH)

    @pl.when(z > 0)
    def _():
        pl.semaphore_signal(barrier, inc=1, device_id=(s, t - 2), device_id_type=MESH)

    pl.semaphore_wait(barrier, 3 + jnp.minimum(z, 1) + jnp.minimum(zs - 1 - z, 1))

    def unit(i):
        return out.at[c, i]

    def right(o, h):
        return remote(out.at[c, o, h], out.at[c, o, h], zsend.at[0, o, h], zrecv.at[o, h], (s, t + 2))

    def left(o, h):
        return remote(out.at[c, o, h], out.at[c, o, h], zsend.at[1, o, h], zrecv.at[o, h], (s, t - 2))

    def to_x(o, i):
        return remote(unit(o), unit(zs + i), send.at[0, i], recv.at[0, i], xdev)

    def to_y(o, i):
        return remote(unit(o), unit(zs + 2 + i), send.at[1, i], recv.at[1, i], ydev)

    def onward_y():
        return remote(unit(zs), unit(zs + 4), send.at[2, 0], recv.at[2, 0], ydev)

    def onward_x():
        return remote(unit(zs + 3), unit(zs + 5), send.at[2, 1], recv.at[2, 1], xdev)

    parts = sib_send.shape[1] // 2
    wide = in_ref.shape[1] // parts

    def with_sib(a, i):
        refs = [out.at[a, i, h, :, pl.ds(f * wide, wide)] for h in range(2) for f in range(parts)]
        return [
            remote(ref, ref, sib_send.at[i, n], sib_recv.at[i, n], sib) for n, ref in enumerate(refs)
        ]

    def to_sib(i):
        for one in with_sib(c, i):
            one.start()

    def sent_sib(i):
        for one in with_sib(c, i):
            one.wait_send()

    def from_sib(i):
        for one in with_sib(1 - c, i):
            one.wait_recv()

    shards = list(enumerate((in_ref, go_ref)))
    locals_ = [pltpu.make_async_copy(ref, out.at[a, z, c], loc.at[a]) for a, ref in shards]
    owns = [remote(ref, out.at[a, z, c], own_send.at[a], own_recv.at[a], sib) for a, ref in shards]
    for one in owns + locals_:
        one.start()
    for one in locals_:
        one.wait()
    for one in owns:
        one.wait_recv()

    def from_z(d, o, onward, near):
        for h in range(2):
            right(o, h).wait_recv()
            onward(o, h)
        if d == 1:

            @pl.when(near)
            def _():
                to_x(o, 1 - r).start()
                to_y(o, 1 - r).start()

        to_sib(o)

    def from_xy(i):
        to_x(z, i).wait_recv()
        pl.when(i == 0)(lambda: onward_y().start())
        to_sib(zs + i)
        to_y(z, i).wait_recv()
        pl.when(i == 1)(lambda: onward_x().start())
        to_sib(zs + 2 + i)

    for h in range(2):
        pl.when(z < zs - 1)(lambda h=h: right(z, h).start())
        pl.when(z > 0)(lambda h=h: left(z, h).start())
    to_x(z, r).start()
    to_y(z, r).start()
    for d in range(1, zs):

        @pl.when(z - d >= 0)
        def _(d=d):
            def on(o, h):
                pl.when(z < zs - 1)(lambda: right(o, h).start())

            from_z(d, z - d, on, r == 1)

        @pl.when(z + d < zs)
        def _(d=d):
            def on(o, h):
                pl.when(z > 0)(lambda: left(o, h).start())

            from_z(d, z + d, on, r == 0)

        if d == 1:
            from_xy(r)
        if d == 2:
            from_xy(1 - r)
    onward_y().wait_recv()
    to_sib(zs + 4)
    onward_x().wait_recv()
    to_sib(zs + 5)

    for one in owns:
        one.wait_send()
    for o in range(zs):
        for h in range(2):
            pl.when((o <= z) & (z < zs - 1))(lambda o=o, h=h: right(o, h).wait_send())
            pl.when((o >= z) & (z > 0))(lambda o=o, h=h: left(o, h).wait_send())

        @pl.when(z != o)
        def _(o=o):
            sent_sib(o)
            from_sib(o)

    for i in range(2):
        to_x(z, i).wait_send()
        to_y(z, i).wait_send()
    onward_y().wait_send()
    onward_x().wait_send()
    for i in range(zs, zs + 6):
        sent_sib(i)
        from_sib(i)


def gather_first(inputs, grad_out, zs):
    rows, features = inputs.shape
    dma = pltpu.SemaphoreType.DMA
    units = zs + 6
    return pl.pallas_call(
        functools.partial(gather_kernel, zs),
        out_shape=jax.ShapeDtypeStruct((2, units, 2, rows, features), inputs.dtype),
        in_specs=[pl.BlockSpec(memory_space=pl.ANY)] * 2,
        out_specs=pl.BlockSpec(memory_space=pl.ANY),
        scratch_shapes=[
            dma((2,)),
            dma((2,)),
            dma((2,)),
            dma((zs, 2)),
            dma((2, zs, 2)),
            dma((3, 2)),
            dma((3, 2)),
            dma((units, 4)),
            dma((units, 4)),
        ],
        compiler_params=pltpu.CompilerParams(collective_id=0, has_side_effects=True),
        name="gather_first",
    )(inputs, grad_out)


def picked_blocks(ref, index, j, slots, width):
    return jnp.concatenate(
        [ref[:, pl.ds(pl.multiple_of(index[j, k] * width, width), width)] for k in range(slots)], axis=1
    )


def forward(xs, gs, up, down):
    slots, width, _ = up.shape
    preact = jnp.dot(xs, up.reshape(slots * width, width), preferred_element_type=jnp.float32)
    down_wide = jnp.concatenate([down[k] for k in range(slots)], axis=1)
    hidden_grad = lax.dot_general(
        gs, down_wide, (((1,), (1,)), ((), ())), preferred_element_type=jnp.float32
    )
    gating = jax.nn.sigmoid(preact)
    pg = (hidden_grad * gating * (1.0 + preact * (1.0 - gating))).astype(jnp.bfloat16)
    return (preact * gating).astype(jnp.bfloat16), pg


def input_kernel(ui, di, pos, x_ref, g_ref, up_ref, down_ref, out_ref, acc):
    j = pl.program_id(0)
    slots, width = up_ref.shape[1], up_ref.shape[2]

    @pl.when(j == 0)
    def _():
        acc[...] = jnp.zeros_like(acc)

    together = up_ref.shape[0]
    terms = []
    for u in range(together):
        row = j * together + u
        xs = picked_blocks(x_ref, ui, row, slots, width)
        gs = picked_blocks(g_ref, di, row, slots, width)
        up = up_ref[u]
        _, pg = forward(xs, gs, up, down_ref[u])
        terms.append(
            lax.dot_general(
                pg,
                up.reshape(slots * width, width),
                (((1,), (1,)), ((), ())),
                preferred_element_type=jnp.float32,
            )
        )
    for u in range(together):
        for k in range(slots):
            where = pl.ds(pl.multiple_of(ui[j * together + u, k] * width, width), width)
            acc[:, where] += terms[u][:, k * width : (k + 1) * width]

    @pl.when(j == pl.num_programs(0) - 1)
    def _():
        out_ref[...] = acc[...].astype(out_ref.dtype)


def input_part(up_index, down_index, pos, both, up_blocks, down_blocks, rows):
    count, slots, width, _ = up_blocks.shape
    features = both.shape[2]
    together = math.gcd(count, 4)
    weight = pl.BlockSpec((together, slots, width, width), lambda j, *_: (j, 0, 0, 0))
    return pl.pallas_call(
        input_kernel,
        out_shape=jax.ShapeDtypeStruct((rows, features), both.dtype),
        grid_spec=pltpu.PrefetchScalarGridSpec(
            num_scalar_prefetch=3,
            grid=(count // together,),
            in_specs=[
                pl.BlockSpec(
                    (None, rows, features), lambda j, *_: (0, 0, 0), pipeline_mode=pl.Buffered(1)
                ),
                pl.BlockSpec(
                    (None, rows, features), lambda j, *_: (1, 0, 0), pipeline_mode=pl.Buffered(1)
                ),
                weight,
                weight,
            ],
            out_specs=pl.BlockSpec((rows, features), lambda j, *_: (0, 0), pipeline_mode=pl.Buffered(1)),
            scratch_shapes=[pltpu.VMEM((rows, features), jnp.float32)],
        ),
        compiler_params=pltpu.CompilerParams(vmem_limit_bytes=60 * MIB),
        cost_estimate=pl.CostEstimate(
            flops=6 * rows * count * slots * width * width,
            bytes_accessed=4 * count * slots * width * width + 6 * rows * features,
            transcendentals=rows * count * width,
        ),
        name="input_part",
    )(up_index, down_index, pos, both, both, up_blocks, down_blocks)


def grads_kernel(
    rows, first, ui, di, have, up_hbm, down_hbm, gup_ref, gdown_ref, far,
    near_x, near_g, up, down, near_xq, near_turned, fill, near_fill, send, recv, sib_send, sib_recv,
):
    s, t, z, c, xdev, ydev, sib = place()
    count, slots, width, _ = up.shape
    share = gup_ref.shape[2]
    mine = pl.ds(pl.multiple_of(s * share, share), share)

    barrier = pltpu.get_barrier_semaphore()
    for dev in (sib, xdev, ydev):
        pl.semaphore_signal(barrier, inc=1, device_id=dev, device_id_type=MESH)
    pl.semaphore_wait(barrier, 3)

    def piece(i):
        return far.at[c, pl.ds(i * rows, rows)]

    def held(i):
        return have.at[c, pl.ds(pl.multiple_of((2 * (1 - z // 2) + i) * rows, rows), rows)]

    def to_x(i):
        return remote(held(i), piece(i), send.at[i], recv.at[i], xdev)

    def to_y(i):
        return remote(held(i), piece(2 + i), send.at[2 + i], recv.at[2 + i], ydev)

    def onward_y():
        return remote(piece(0), piece(4), send.at[4], recv.at[4], ydev)

    def onward_x():
        return remote(piece(3), piece(5), send.at[5], recv.at[5], xdev)

    def to_sib(i):
        return remote(piece(i), piece(i), sib_send.at[i], sib_recv.at[i], sib)

    def from_sib(i):
        other = far.at[1 - c, pl.ds(i * rows, rows)]
        return remote(other, other, sib_send.at[i], sib_recv.at[i], sib)

    sends = (to_x(0), to_x(1), to_y(0), to_y(1), onward_y(), onward_x())
    for i in (0, 3, 1, 2):
        sends[i].start()
    fills = [
        pltpu.make_async_copy(src, dst, fill.at[i])
        for i, (src, dst) in enumerate(((up_hbm, up), (down_hbm, down)))
    ]

    def columns(src, a, dst, sems, b):
        where = pl.ds(pl.multiple_of(b * width, width), width)
        return pltpu.make_async_copy(src.at[a, :, where], dst.at[b], sems.at[a, b])

    def start_columns(src, x, g, sems):
        def one(b, carry):
            columns(src, 0, x, sems, b).start()
            columns(src, 1, g, sems, b).start()
            return carry

        lax.fori_loop(0, x.shape[0], one, 0)

    def wait_columns(src, x, g, sems):
        def one(b, carry):
            columns(src, 0, x, sems, b).wait()
            columns(src, 1, g, sems, b).wait()
            return carry

        lax.fori_loop(0, x.shape[0], one, 0)

    start_columns(have, near_x, near_g, near_fill)
    for one in fills:
        one.start()

    def arrived(i):
        sends[i].wait_recv()

    def turn(x, xq, turned):
        together = turned.shape[0]

        def one(b, carry):
            for u in range(together):
                block = b * together + u
                turned[u] = x[block].T
                xq[block] = turned[u, mine, :]
            return carry

        lax.fori_loop(0, xq.shape[0] // together, one, 0)

    def add(x, g, xq, turned, start, stop):
        together = turned.shape[0]

        def one(j, carry):
            for u in range(together):
                row = j * together + u
                xs = jnp.concatenate([x[ui[row, k]] for k in range(slots)], axis=1)
                gs = jnp.concatenate([g[di[row, k]] for k in range(slots)], axis=1)
                activated, pg = forward(xs, gs, up[row], down[row])
                quarter = jnp.concatenate([xq[ui[row, k]] for k in range(slots)], axis=0)
                gup = jnp.dot(quarter, pg, preferred_element_type=jnp.float32)
                gup_ref[row] = gup.reshape(slots, share, width)
                turned[u] = activated.T
                gdown = jnp.dot(turned[u, mine, :], gs, preferred_element_type=jnp.float32)
                for k in range(slots):
                    gdown_ref[row, k] = gdown[:, k * width : (k + 1) * width]
            return carry

        lax.fori_loop(start // together, stop // together, one, 0)

    wait_columns(have, near_x, near_g, near_fill)
    turn(near_x, near_xq, near_turned)
    for one in fills:
        one.wait()
    add(near_x, near_g, near_xq, near_turned, 0, first)
    arrived(0)
    sends[4].start()
    to_sib(0).start()
    arrived(3)
    sends[5].start()
    to_sib(3).start()
    add(near_x, near_g, near_xq, near_turned, first, count)
    for i in (1, 2, 4, 5):
        arrived(i)
        to_sib(i).start()
    for i in range(6):
        from_sib(i).wait_recv()
    for i in range(6):
        sends[i].wait_send()
        to_sib(i).wait_send()


def near_grads(up_index, down_index, have, up_blocks, down_blocks, rows, share):
    count, slots, width, _ = up_blocks.shape
    _, tokens, features = have.shape
    dtype = have.dtype
    together = math.gcd(count, 4)
    first = count // 2 // together * together
    blocks = features // width
    shape = jax.ShapeDtypeStruct((count, slots, share, width), jnp.float32)
    dma = pltpu.SemaphoreType.DMA
    vmem = pltpu.VMEM
    return pl.pallas_call(
        functools.partial(grads_kernel, rows, first),
        out_shape=[shape, shape, jax.ShapeDtypeStruct((2, 6 * rows, features), dtype)],
        in_specs=[pl.BlockSpec(memory_space=pltpu.SMEM)] * 2 + [pl.BlockSpec(memory_space=pl.ANY)] * 3,
        out_specs=[pl.BlockSpec(memory_space=vmem)] * 2 + [pl.BlockSpec(memory_space=pl.ANY)],
        scratch_shapes=[
            vmem((blocks, tokens, width), dtype),
            vmem((blocks, tokens, width), dtype),
            vmem(up_blocks.shape, dtype),
            vmem(down_blocks.shape, dtype),
            vmem((blocks, share, tokens), dtype),
            vmem((together, width, tokens), dtype),
            dma((2,)),
            dma((2, blocks)),
            dma((6,)),
            dma((6,)),
            dma((6,)),
            dma((6,)),
        ],
        compiler_params=pltpu.CompilerParams(
            collective_id=1, has_side_effects=True, vmem_limit_bytes=60 * MIB
        ),
        cost_estimate=pl.CostEstimate(
            flops=6 * tokens * count * slots * width * width,
            bytes_accessed=6 * count * slots * width * width + 6 * tokens * features,
            transcendentals=tokens * count * width,
        ),
        name="near_grads",
    )(up_index, down_index, have, up_blocks, down_blocks)


def far_kernel(
    factor, ui, di, pos, x_ref, g_ref, up_ref, down_ref, gup_in, gdown_in, gup_ref, gdown_ref, xq, turned
):
    j = pl.program_id(0)
    together, slots, width, _ = up_ref.shape
    share = gup_ref.shape[2]
    mine = pl.ds(pl.multiple_of(pos[0] * share, share), share)

    @pl.when(j == 0)
    def _():
        def one(b, carry):
            for u in range(together):
                block = b * together + u
                turned[u] = x_ref[:, pl.ds(pl.multiple_of(block * width, width), width)].T
                xq[block] = turned[u, mine, :]
            return carry

        lax.fori_loop(0, xq.shape[0] // together, one, 0)

    for u in range(together):
        row = j * together + u
        xs = picked_blocks(x_ref, ui, row, slots, width)
        gs = picked_blocks(g_ref, di, row, slots, width)
        activated, pg = forward(xs, gs, up_ref[u], down_ref[u])
        quarter = jnp.concatenate([xq[ui[row, k]] for k in range(slots)], axis=0)
        gup = jnp.dot(quarter, pg, preferred_element_type=jnp.float32).reshape(slots, share, width)
        gup_ref[u] = ((gup_in[u] + gup) * factor).astype(gup_ref.dtype)
        turned[u] = activated.T
        gdown = jnp.dot(turned[u, mine, :], gs, preferred_element_type=jnp.float32)
        for k in range(slots):
            part = gdown[:, k * width : (k + 1) * width]
            gdown_ref[u, k] = ((gdown_in[u, k] + part) * factor).astype(gdown_ref.dtype)


def far_grads(up_index, down_index, pos, far, up_blocks, down_blocks, gup, gdown, factor):
    count, slots, width, _ = up_blocks.shape
    share = gup.shape[2]
    _, tokens, features = far.shape
    together = math.gcd(count, 4)
    weight = pl.BlockSpec((together, slots, width, width), lambda j, *_: (j, 0, 0, 0))
    result = pl.BlockSpec((together, slots, share, width), lambda j, *_: (j, 0, 0, 0))
    shape = jax.ShapeDtypeStruct((count, slots, share, width), far.dtype)
    once = pl.Buffered(1)
    return pl.pallas_call(
        functools.partial(far_kernel, factor),
        out_shape=[shape, shape],
        grid_spec=pltpu.PrefetchScalarGridSpec(
            num_scalar_prefetch=3,
            grid=(count // together,),
            in_specs=[
                pl.BlockSpec((None, tokens, features), lambda j, *_: (0, 0, 0), pipeline_mode=once),
                pl.BlockSpec((None, tokens, features), lambda j, *_: (1, 0, 0), pipeline_mode=once),
                weight,
                weight,
                result,
                result,
            ],
            out_specs=[result, result],
            scratch_shapes=[
                pltpu.VMEM((features // width, share, tokens), far.dtype),
                pltpu.VMEM((together, width, tokens), far.dtype),
            ],
        ),
        compiler_params=pltpu.CompilerParams(vmem_limit_bytes=60 * MIB),
        cost_estimate=pl.CostEstimate(
            flops=6 * tokens * count * slots * width * width,
            bytes_accessed=6 * count * slots * width * width + 4 * tokens * features,
            transcendentals=tokens * count * width,
        ),
        name="far_grads",
    )(up_index, down_index, pos, far, far, up_blocks, down_blocks, gup, gdown)


def local_all_tokens(inputs, grad_out, up_blocks, up_index, down_blocks, down_index):
    tensor_count = lax.axis_size("tensor")
    seq_count = lax.axis_size("seq")
    rows_here, features = inputs.shape
    block = up_blocks.shape[2]
    group_rows = rows_here * tensor_count
    factor = 1.0 / math.sqrt(group_rows * seq_count)
    have = gather_first(inputs, grad_out, tensor_count // 2)
    have = have.reshape(2, -1, features)
    pos = lax.axis_index("seq").astype(jnp.int32).reshape(1)
    part = input_part(up_index, down_index, pos, have, up_blocks, down_blocks, group_rows)
    pieces = part.reshape(tensor_count, rows_here, features)
    received = lax.all_to_all(pieces, "tensor", split_axis=0, concat_axis=0, tiled=True)
    near_up, near_down, far = near_grads(
        up_index, down_index, have, up_blocks, down_blocks, 2 * rows_here, block // seq_count
    )
    grad_up, grad_down = far_grads(
        up_index, down_index, pos, far, up_blocks, down_blocks, near_up, near_down, factor
    )
    grad_in = jnp.sum(received.astype(jnp.float32), axis=0).astype(jnp.bfloat16)
    return (grad_in, grad_up, grad_down)


def local(inputs, grad_out, up_blocks, up_index, down_blocks, down_index):
    tensor_count = lax.axis_size("tensor")
    seq_count = lax.axis_size("seq")
    rows_here, features = inputs.shape
    local_blocks, slots, block, _ = up_blocks.shape
    blocks_wide = features // block
    group_rows = rows_here * tensor_count
    factor = 1.0 / math.sqrt(group_rows * seq_count)
    flat_index = up_index.reshape(-1)
    in_rows = lax.all_gather(inputs, "tensor", axis=0, tiled=True)
    grad_rows = lax.all_gather(grad_out, "tensor", axis=0, tiled=True)
    piece_rows = in_rows.shape[0]
    picked = jnp.take(in_rows.reshape(piece_rows, blocks_wide, block), up_index, axis=1)
    picked_grad = jnp.take(grad_rows.reshape(piece_rows, blocks_wide, block), down_index, axis=1)
    preact = jnp.einsum("rjkc,jkch->rjh", picked, up_blocks, preferred_element_type=jnp.float32)
    hidden_grad = jnp.einsum(
        "rjko,jkho->rjh", picked_grad, down_blocks, preferred_element_type=jnp.float32
    )
    gating = jax.nn.sigmoid(preact)
    activated = (preact * gating).astype(jnp.bfloat16)
    preact_grad = (hidden_grad * gating * (1.0 + preact * (1.0 - gating))).astype(jnp.bfloat16)
    up_sum = jnp.einsum("rjkc,rjh->jkch", picked, preact_grad, preferred_element_type=jnp.float32)
    down_sum = jnp.einsum(
        "rjh,rjko->jkho", activated, picked_grad, preferred_element_type=jnp.float32
    )
    contrib = jnp.einsum(
        "rjh,jkch->rjkc", preact_grad, up_blocks, preferred_element_type=jnp.float32
    )
    contrib = contrib.reshape(piece_rows, local_blocks * slots, block)
    partial_value = (
        jnp.zeros((piece_rows, blocks_wide, block), jnp.float32).at[:, flat_index].add(contrib)
    )
    input_grad = partial_value
    up_sum, down_sum, input_grad = (up_sum, down_sum, input_grad)
    share = block // seq_count
    up_part = (
        (up_sum * factor).astype(jnp.bfloat16).reshape(local_blocks, slots, seq_count, share, block)
    )
    down_part = (
        (down_sum * factor)
        .astype(jnp.bfloat16)
        .reshape(local_blocks, slots, seq_count, share, block)
    )
    up_recv, down_recv = (
        lax.all_to_all(up_part, "seq", split_axis=2, concat_axis=2, tiled=True),
        lax.all_to_all(down_part, "seq", split_axis=2, concat_axis=2, tiled=True),
    )
    grad_up = jnp.sum(up_recv.astype(jnp.float32), axis=2).astype(jnp.bfloat16)
    grad_down = jnp.sum(down_recv.astype(jnp.float32), axis=2).astype(jnp.bfloat16)
    partial_rows = input_grad.reshape(group_rows, features).astype(jnp.bfloat16)
    pieces = partial_rows.reshape(tensor_count, rows_here, features)
    received = lax.all_to_all(pieces, "tensor", split_axis=0, concat_axis=0, tiled=True)
    grad_in = jnp.sum(received.astype(jnp.float32), axis=0).astype(jnp.bfloat16)
    return (grad_in, grad_up, grad_down)

def solution(mesh):
    gathers = mesh.shape["seq"] == 4 and mesh.shape["tensor"] == 8
    return jax.shard_map(
        local_all_tokens if gathers else local,
        mesh=mesh,
        in_specs=(
            P(("seq", "tensor"), None),
            P(("seq", "tensor"), None),
            P("tensor", None, None, None),
            P("tensor", None),
            P("tensor", None, None, None),
            P("tensor", None),
        ),
        out_specs=(
            P(("seq", "tensor"), None),
            P("tensor", None, "seq", None),
            P("tensor", None, "seq", None),
        ),
        check_vma=False,
    )
```

```python
import functools
import math

import jax
import jax.numpy as jnp
from jax import lax
from jax.experimental import pallas as pl
from jax.experimental.pallas import tpu as pltpu
from jax.sharding import PartitionSpec as P

MESH = pl.DeviceIdType.MESH
MIB = 1024 * 1024


def place():
    s, t = lax.axis_index("seq"), lax.axis_index("tensor")
    z, c = t // 2, t % 2
    x, y = s % 2, s // 2
    xn, yn = y * 2 + (1 - x), (1 - y) * 2 + x
    return s, t, z, c, (xn, t), (yn, t), (s, z * 2 + (1 - c))


def remote(src, dst, send, recv, dev):
    return pltpu.make_async_remote_copy(
        src_ref=src, dst_ref=dst, send_sem=send, recv_sem=recv, device_id=dev, device_id_type=MESH
    )


def gather_kernel(
    zs, in_ref, go_ref, out, loc, own_send, own_recv, zrecv, zsend, recv, send, sib_send, sib_recv
):
    s, t, z, c, xdev, ydev, sib = place()
    r = z % 2
    mate = z + 1 - 2 * r

    barrier = pltpu.get_barrier_semaphore()
    for dev in (sib, xdev, ydev):
        pl.semaphore_signal(barrier, inc=1, device_id=dev, device_id_type=MESH)

    @pl.when(z < zs - 1)
    def _():
        pl.semaphore_signal(barrier, inc=1, device_id=(s, t + 2), device_id_type=MESH)

    @pl.when(z > 0)
    def _():
        pl.semaphore_signal(barrier, inc=1, device_id=(s, t - 2), device_id_type=MESH)

    pl.semaphore_wait(barrier, 3 + jnp.minimum(z, 1) + jnp.minimum(zs - 1 - z, 1))

    def unit(i):
        return out.at[c, i]

    def right(o, h):
        return remote(out.at[c, o, h], out.at[c, o, h], zsend.at[0, o, h], zrecv.at[o, h], (s, t + 2))

    def left(o, h):
        return remote(out.at[c, o, h], out.at[c, o, h], zsend.at[1, o, h], zrecv.at[o, h], (s, t - 2))

    def to_x(o, i):
        return remote(unit(o), unit(zs + i), send.at[0, i], recv.at[0, i], xdev)

    def to_y(o, i):
        return remote(unit(o), unit(zs + 2 + i), send.at[1, i], recv.at[1, i], ydev)

    def onward_y():
        return remote(unit(zs), unit(zs + 4), send.at[2, 0], recv.at[2, 0], ydev)

    def onward_x():
        return remote(unit(zs + 3), unit(zs + 5), send.at[2, 1], recv.at[2, 1], xdev)

    parts = sib_send.shape[1] // 2
    wide = in_ref.shape[1] // parts

    def with_sib(a, i):
        refs = [out.at[a, i, h, :, pl.ds(f * wide, wide)] for h in range(2) for f in range(parts)]
        return [
            remote(ref, ref, sib_send.at[i, n], sib_recv.at[i, n], sib) for n, ref in enumerate(refs)
        ]

    def to_sib(i):
        for one in with_sib(c, i):
            one.start()

    def sent_sib(i):
        for one in with_sib(c, i):
            one.wait_send()

    def from_sib(i):
        for one in with_sib(1 - c, i):
            one.wait_recv()

    shards = list(enumerate((in_ref, go_ref)))
    locals_ = [pltpu.make_async_copy(ref, out.at[a, z, c], loc.at[a]) for a, ref in shards]
    owns = [remote(ref, out.at[a, z, c], own_send.at[a], own_recv.at[a], sib) for a, ref in shards]
    for one in owns + locals_:
        one.start()
    for one in locals_:
        one.wait()
    for one in owns:
        one.wait_recv()

    def from_z(d, o, onward, near):
        for h in range(2):
            right(o, h).wait_recv()
            onward(o, h)
        if d == 1:

            @pl.when(near)
            def _():
                to_x(o, 1 - r).start()
                to_y(o, 1 - r).start()

        to_sib(o)

    def from_xy(i):
        to_x(z, i).wait_recv()
        pl.when(i == 0)(lambda: onward_y().start())
        to_sib(zs + i)
        to_y(z, i).wait_recv()
        pl.when(i == 1)(lambda: onward_x().start())
        to_sib(zs + 2 + i)

    for h in range(2):
        pl.when(z < zs - 1)(lambda h=h: right(z, h).start())
        pl.when(z > 0)(lambda h=h: left(z, h).start())
    to_x(z, r).start()
    to_y(z, r).start()
    for d in range(1, zs):

        @pl.when(z - d >= 0)
        def _(d=d):
            def on(o, h):
                pl.when(z < zs - 1)(lambda: right(o, h).start())

            from_z(d, z - d, on, r == 1)

        @pl.when(z + d < zs)
        def _(d=d):
            def on(o, h):
                pl.when(z > 0)(lambda: left(o, h).start())

            from_z(d, z + d, on, r == 0)

        if d == 1:
            from_xy(r)
        if d == 2:
            from_xy(1 - r)
    onward_y().wait_recv()
    to_sib(zs + 4)
    onward_x().wait_recv()
    to_sib(zs + 5)

    for one in owns:
        one.wait_send()
    for o in range(zs):
        for h in range(2):
            pl.when((o <= z) & (z < zs - 1))(lambda o=o, h=h: right(o, h).wait_send())
            pl.when((o >= z) & (z > 0))(lambda o=o, h=h: left(o, h).wait_send())

        @pl.when(z != o)
        def _(o=o):
            sent_sib(o)
            from_sib(o)

    for i in range(2):
        to_x(z, i).wait_send()
        to_y(z, i).wait_send()
    onward_y().wait_send()
    onward_x().wait_send()
    for i in range(zs, zs + 6):
        sent_sib(i)
        from_sib(i)


def gather_first(inputs, grad_out, zs):
    rows, features = inputs.shape
    dma = pltpu.SemaphoreType.DMA
    units = zs + 6
    return pl.pallas_call(
        functools.partial(gather_kernel, zs),
        out_shape=jax.ShapeDtypeStruct((2, units, 2, rows, features), inputs.dtype),
        in_specs=[pl.BlockSpec(memory_space=pl.ANY)] * 2,
        out_specs=pl.BlockSpec(memory_space=pl.ANY),
        scratch_shapes=[
            dma((2,)),
            dma((2,)),
            dma((2,)),
            dma((zs, 2)),
            dma((2, zs, 2)),
            dma((3, 2)),
            dma((3, 2)),
            dma((units, 4)),
            dma((units, 4)),
        ],
        compiler_params=pltpu.CompilerParams(collective_id=0, has_side_effects=True),
        name="gather_first",
    )(inputs, grad_out)


def picked_blocks(ref, index, j, slots, width):
    return jnp.concatenate(
        [ref[:, pl.ds(pl.multiple_of(index[j, k] * width, width), width)] for k in range(slots)], axis=1
    )


def forward(xs, gs, up, down):
    slots, width, _ = up.shape
    preact = jnp.dot(xs, up.reshape(slots * width, width), preferred_element_type=jnp.float32)
    down_wide = jnp.concatenate([down[k] for k in range(slots)], axis=1)
    hidden_grad = lax.dot_general(
        gs, down_wide, (((1,), (1,)), ((), ())), preferred_element_type=jnp.float32
    )
    gating = jax.nn.sigmoid(preact)
    pg = (hidden_grad * gating * (1.0 + preact * (1.0 - gating))).astype(jnp.bfloat16)
    return (preact * gating).astype(jnp.bfloat16), pg


def input_kernel(ui, di, pos, x_ref, g_ref, up_ref, down_ref, out_ref, acc):
    j = pl.program_id(0)
    slots, width = up_ref.shape[1], up_ref.shape[2]

    @pl.when(j == 0)
    def _():
        acc[...] = jnp.zeros_like(acc)

    together = up_ref.shape[0]
    terms = []
    for u in range(together):
        row = j * together + u
        xs = picked_blocks(x_ref, ui, row, slots, width)
        gs = picked_blocks(g_ref, di, row, slots, width)
        up = up_ref[u]
        _, pg = forward(xs, gs, up, down_ref[u])
        terms.append(
            lax.dot_general(
                pg,
                up.reshape(slots * width, width),
                (((1,), (1,)), ((), ())),
                preferred_element_type=jnp.float32,
            )
        )
    for u in range(together):
        for k in range(slots):
            where = pl.ds(pl.multiple_of(ui[j * together + u, k] * width, width), width)
            acc[:, where] += terms[u][:, k * width : (k + 1) * width]

    @pl.when(j == pl.num_programs(0) - 1)
    def _():
        out_ref[...] = acc[...].astype(out_ref.dtype)


def input_part(up_index, down_index, pos, both, up_blocks, down_blocks, rows):
    count, slots, width, _ = up_blocks.shape
    features = both.shape[2]
    together = math.gcd(count, 4)
    weight = pl.BlockSpec((together, slots, width, width), lambda j, *_: (j, 0, 0, 0))
    return pl.pallas_call(
        input_kernel,
        out_shape=jax.ShapeDtypeStruct((rows, features), both.dtype),
        grid_spec=pltpu.PrefetchScalarGridSpec(
            num_scalar_prefetch=3,
            grid=(count // together,),
            in_specs=[
                pl.BlockSpec(
                    (None, rows, features), lambda j, *_: (0, 0, 0), pipeline_mode=pl.Buffered(1)
                ),
                pl.BlockSpec(
                    (None, rows, features), lambda j, *_: (1, 0, 0), pipeline_mode=pl.Buffered(1)
                ),
                weight,
                weight,
            ],
            out_specs=pl.BlockSpec((rows, features), lambda j, *_: (0, 0), pipeline_mode=pl.Buffered(1)),
            scratch_shapes=[pltpu.VMEM((rows, features), jnp.float32)],
        ),
        compiler_params=pltpu.CompilerParams(vmem_limit_bytes=60 * MIB),
        cost_estimate=pl.CostEstimate(
            flops=6 * rows * count * slots * width * width,
            bytes_accessed=4 * count * slots * width * width + 6 * rows * features,
            transcendentals=rows * count * width,
        ),
        name="input_part",
    )(up_index, down_index, pos, both, both, up_blocks, down_blocks)


def grads_kernel(
    rows, first, ui, di, have, up_hbm, down_hbm, gup_ref, gdown_ref, far,
    near_x, near_g, up, down, near_xq, near_turned, fill, near_fill, send, recv, sib_send, sib_recv,
):
    s, t, z, c, xdev, ydev, sib = place()
    count, slots, width, _ = up.shape
    share = gup_ref.shape[2]
    mine = pl.ds(pl.multiple_of(s * share, share), share)

    barrier = pltpu.get_barrier_semaphore()
    for dev in (sib, xdev, ydev):
        pl.semaphore_signal(barrier, inc=1, device_id=dev, device_id_type=MESH)
    pl.semaphore_wait(barrier, 3)

    def piece(i):
        return far.at[c, pl.ds(i * rows, rows)]

    def held(i):
        return have.at[c, pl.ds(pl.multiple_of((2 * (1 - z // 2) + i) * rows, rows), rows)]

    def to_x(i):
        return remote(held(i), piece(i), send.at[i], recv.at[i], xdev)

    def to_y(i):
        return remote(held(i), piece(2 + i), send.at[2 + i], recv.at[2 + i], ydev)

    def onward_y():
        return remote(piece(0), piece(4), send.at[4], recv.at[4], ydev)

    def onward_x():
        return remote(piece(3), piece(5), send.at[5], recv.at[5], xdev)

    def to_sib(i):
        return remote(piece(i), piece(i), sib_send.at[i], sib_recv.at[i], sib)

    def from_sib(i):
        other = far.at[1 - c, pl.ds(i * rows, rows)]
        return remote(other, other, sib_send.at[i], sib_recv.at[i], sib)

    sends = (to_x(0), to_x(1), to_y(0), to_y(1), onward_y(), onward_x())
    for i in (0, 3):
        sends[i].start()
    fills = [
        pltpu.make_async_copy(src, dst, fill.at[i])
        for i, (src, dst) in enumerate(((up_hbm, up), (down_hbm, down)))
    ]

    def columns(src, a, dst, sems, b):
        where = pl.ds(pl.multiple_of(b * width, width), width)
        return pltpu.make_async_copy(src.at[a, :, where], dst.at[b], sems.at[a, b])

    def start_columns(src, x, g, sems):
        def one(b, carry):
            columns(src, 0, x, sems, b).start()
            columns(src, 1, g, sems, b).start()
            return carry

        lax.fori_loop(0, x.shape[0], one, 0)

    def wait_columns(src, x, g, sems):
        def one(b, carry):
            columns(src, 0, x, sems, b).wait()
            columns(src, 1, g, sems, b).wait()
            return carry

        lax.fori_loop(0, x.shape[0], one, 0)

    start_columns(have, near_x, near_g, near_fill)
    for one in fills:
        one.start()

    def arrived(i):
        sends[i].wait_recv()

    def turn(x, xq, turned):
        together = turned.shape[0]

        def one(b, carry):
            for u in range(together):
                block = b * together + u
                turned[u] = x[block].T
                xq[block] = turned[u, mine, :]
            return carry

        lax.fori_loop(0, xq.shape[0] // together, one, 0)

    def add(x, g, xq, turned, start, stop):
        together = turned.shape[0]

        def one(j, carry):
            for u in range(together):
                row = j * together + u
                xs = jnp.concatenate([x[ui[row, k]] for k in range(slots)], axis=1)
                gs = jnp.concatenate([g[di[row, k]] for k in range(slots)], axis=1)
                activated, pg = forward(xs, gs, up[row], down[row])
                quarter = jnp.concatenate([xq[ui[row, k]] for k in range(slots)], axis=0)
                gup = jnp.dot(quarter, pg, preferred_element_type=jnp.float32)
                gup_ref[row] = gup.reshape(slots, share, width)
                turned[u] = activated.T
                gdown = jnp.dot(turned[u, mine, :], gs, preferred_element_type=jnp.float32)
                for k in range(slots):
                    gdown_ref[row, k] = gdown[:, k * width : (k + 1) * width]
            return carry

        lax.fori_loop(start // together, stop // together, one, 0)

    wait_columns(have, near_x, near_g, near_fill)
    for i in (1, 2):
        sends[i].start()
    turn(near_x, near_xq, near_turned)
    for one in fills:
        one.wait()
    add(near_x, near_g, near_xq, near_turned, 0, first)
    arrived(0)
    sends[4].start()
    to_sib(0).start()
    arrived(3)
    sends[5].start()
    to_sib(3).start()
    add(near_x, near_g, near_xq, near_turned, first, count)
    for i in (1, 2, 4, 5):
        arrived(i)
        to_sib(i).start()
    for i in range(6):
        from_sib(i).wait_recv()
    for i in range(6):
        sends[i].wait_send()
        to_sib(i).wait_send()


def near_grads(up_index, down_index, have, up_blocks, down_blocks, rows, share):
    count, slots, width, _ = up_blocks.shape
    _, tokens, features = have.shape
    dtype = have.dtype
    together = math.gcd(count, 4)
    first = count // 2 // together * together
    blocks = features // width
    shape = jax.ShapeDtypeStruct((count, slots, share, width), jnp.float32)
    dma = pltpu.SemaphoreType.DMA
    vmem = pltpu.VMEM
    return pl.pallas_call(
        functools.partial(grads_kernel, rows, first),
        out_shape=[shape, shape, jax.ShapeDtypeStruct((2, 6 * rows, features), dtype)],
        in_specs=[pl.BlockSpec(memory_space=pltpu.SMEM)] * 2 + [pl.BlockSpec(memory_space=pl.ANY)] * 3,
        out_specs=[pl.BlockSpec(memory_space=vmem)] * 2 + [pl.BlockSpec(memory_space=pl.ANY)],
        scratch_shapes=[
            vmem((blocks, tokens, width), dtype),
            vmem((blocks, tokens, width), dtype),
            vmem(up_blocks.shape, dtype),
            vmem(down_blocks.shape, dtype),
            vmem((blocks, share, tokens), dtype),
            vmem((together, width, tokens), dtype),
            dma((2,)),
            dma((2, blocks)),
            dma((6,)),
            dma((6,)),
            dma((6,)),
            dma((6,)),
        ],
        compiler_params=pltpu.CompilerParams(
            collective_id=1, has_side_effects=True, vmem_limit_bytes=60 * MIB
        ),
        cost_estimate=pl.CostEstimate(
            flops=6 * tokens * count * slots * width * width,
            bytes_accessed=6 * count * slots * width * width + 6 * tokens * features,
            transcendentals=tokens * count * width,
        ),
        name="near_grads",
    )(up_index, down_index, have, up_blocks, down_blocks)


def far_kernel(
    factor, ui, di, pos, x_ref, g_ref, up_ref, down_ref, gup_in, gdown_in, gup_ref, gdown_ref, xq, turned
):
    j = pl.program_id(0)
    together, slots, width, _ = up_ref.shape
    share = gup_ref.shape[2]
    mine = pl.ds(pl.multiple_of(pos[0] * share, share), share)

    @pl.when(j == 0)
    def _():
        def one(b, carry):
            for u in range(together):
                block = b * together + u
                turned[u] = x_ref[:, pl.ds(pl.multiple_of(block * width, width), width)].T
                xq[block] = turned[u, mine, :]
            return carry

        lax.fori_loop(0, xq.shape[0] // together, one, 0)

    for u in range(together):
        row = j * together + u
        xs = picked_blocks(x_ref, ui, row, slots, width)
        gs = picked_blocks(g_ref, di, row, slots, width)
        activated, pg = forward(xs, gs, up_ref[u], down_ref[u])
        quarter = jnp.concatenate([xq[ui[row, k]] for k in range(slots)], axis=0)
        gup = jnp.dot(quarter, pg, preferred_element_type=jnp.float32).reshape(slots, share, width)
        gup_ref[u] = ((gup_in[u] + gup) * factor).astype(gup_ref.dtype)
        turned[u] = activated.T
        gdown = jnp.dot(turned[u, mine, :], gs, preferred_element_type=jnp.float32)
        for k in range(slots):
            part = gdown[:, k * width : (k + 1) * width]
            gdown_ref[u, k] = ((gdown_in[u, k] + part) * factor).astype(gdown_ref.dtype)


def far_grads(up_index, down_index, pos, far, up_blocks, down_blocks, gup, gdown, factor):
    count, slots, width, _ = up_blocks.shape
    share = gup.shape[2]
    _, tokens, features = far.shape
    together = math.gcd(count, 4)
    weight = pl.BlockSpec((together, slots, width, width), lambda j, *_: (j, 0, 0, 0))
    result = pl.BlockSpec((together, slots, share, width), lambda j, *_: (j, 0, 0, 0))
    shape = jax.ShapeDtypeStruct((count, slots, share, width), far.dtype)
    once = pl.Buffered(1)
    return pl.pallas_call(
        functools.partial(far_kernel, factor),
        out_shape=[shape, shape],
        grid_spec=pltpu.PrefetchScalarGridSpec(
            num_scalar_prefetch=3,
            grid=(count // together,),
            in_specs=[
                pl.BlockSpec((None, tokens, features), lambda j, *_: (0, 0, 0), pipeline_mode=once),
                pl.BlockSpec((None, tokens, features), lambda j, *_: (1, 0, 0), pipeline_mode=once),
                weight,
                weight,
                result,
                result,
            ],
            out_specs=[result, result],
            scratch_shapes=[
                pltpu.VMEM((features // width, share, tokens), far.dtype),
                pltpu.VMEM((together, width, tokens), far.dtype),
            ],
        ),
        compiler_params=pltpu.CompilerParams(vmem_limit_bytes=60 * MIB),
        cost_estimate=pl.CostEstimate(
            flops=6 * tokens * count * slots * width * width,
            bytes_accessed=6 * count * slots * width * width + 4 * tokens * features,
            transcendentals=tokens * count * width,
        ),
        name="far_grads",
    )(up_index, down_index, pos, far, far, up_blocks, down_blocks, gup, gdown)


def local_all_tokens(inputs, grad_out, up_blocks, up_index, down_blocks, down_index):
    tensor_count = lax.axis_size("tensor")
    seq_count = lax.axis_size("seq")
    rows_here, features = inputs.shape
    block = up_blocks.shape[2]
    group_rows = rows_here * tensor_count
    factor = 1.0 / math.sqrt(group_rows * seq_count)
    have = gather_first(inputs, grad_out, tensor_count // 2)
    have = have.reshape(2, -1, features)
    pos = lax.axis_index("seq").astype(jnp.int32).reshape(1)
    part = input_part(up_index, down_index, pos, have, up_blocks, down_blocks, group_rows)
    pieces = part.reshape(tensor_count, rows_here, features)
    received = lax.all_to_all(pieces, "tensor", split_axis=0, concat_axis=0, tiled=True)
    near_up, near_down, far = near_grads(
        up_index, down_index, have, up_blocks, down_blocks, 2 * rows_here, block // seq_count
    )
    grad_up, grad_down = far_grads(
        up_index, down_index, pos, far, up_blocks, down_blocks, near_up, near_down, factor
    )
    grad_in = jnp.sum(received.astype(jnp.float32), axis=0).astype(jnp.bfloat16)
    return (grad_in, grad_up, grad_down)


def local(inputs, grad_out, up_blocks, up_index, down_blocks, down_index):
    tensor_count = lax.axis_size("tensor")
    seq_count = lax.axis_size("seq")
    rows_here, features = inputs.shape
    local_blocks, slots, block, _ = up_blocks.shape
    blocks_wide = features // block
    group_rows = rows_here * tensor_count
    factor = 1.0 / math.sqrt(group_rows * seq_count)
    flat_index = up_index.reshape(-1)
    in_rows = lax.all_gather(inputs, "tensor", axis=0, tiled=True)
    grad_rows = lax.all_gather(grad_out, "tensor", axis=0, tiled=True)
    piece_rows = in_rows.shape[0]
    picked = jnp.take(in_rows.reshape(piece_rows, blocks_wide, block), up_index, axis=1)
    picked_grad = jnp.take(grad_rows.reshape(piece_rows, blocks_wide, block), down_index, axis=1)
    preact = jnp.einsum("rjkc,jkch->rjh", picked, up_blocks, preferred_element_type=jnp.float32)
    hidden_grad = jnp.einsum(
        "rjko,jkho->rjh", picked_grad, down_blocks, preferred_element_type=jnp.float32
    )
    gating = jax.nn.sigmoid(preact)
    activated = (preact * gating).astype(jnp.bfloat16)
    preact_grad = (hidden_grad * gating * (1.0 + preact * (1.0 - gating))).astype(jnp.bfloat16)
    up_sum = jnp.einsum("rjkc,rjh->jkch", picked, preact_grad, preferred_element_type=jnp.float32)
    down_sum = jnp.einsum(
        "rjh,rjko->jkho", activated, picked_grad, preferred_element_type=jnp.float32
    )
    contrib = jnp.einsum(
        "rjh,jkch->rjkc", preact_grad, up_blocks, preferred_element_type=jnp.float32
    )
    contrib = contrib.reshape(piece_rows, local_blocks * slots, block)
    partial_value = (
        jnp.zeros((piece_rows, blocks_wide, block), jnp.float32).at[:, flat_index].add(contrib)
    )
    input_grad = partial_value
    up_sum, down_sum, input_grad = (up_sum, down_sum, input_grad)
    share = block // seq_count
    up_part = (
        (up_sum * factor).astype(jnp.bfloat16).reshape(local_blocks, slots, seq_count, share, block)
    )
    down_part = (
        (down_sum * factor)
        .astype(jnp.bfloat16)
        .reshape(local_blocks, slots, seq_count, share, block)
    )
    up_recv, down_recv = (
        lax.all_to_all(up_part, "seq", split_axis=2, concat_axis=2, tiled=True),
        lax.all_to_all(down_part, "seq", split_axis=2, concat_axis=2, tiled=True),
    )
    grad_up = jnp.sum(up_recv.astype(jnp.float32), axis=2).astype(jnp.bfloat16)
    grad_down = jnp.sum(down_recv.astype(jnp.float32), axis=2).astype(jnp.bfloat16)
    partial_rows = input_grad.reshape(group_rows, features).astype(jnp.bfloat16)
    pieces = partial_rows.reshape(tensor_count, rows_here, features)
    received = lax.all_to_all(pieces, "tensor", split_axis=0, concat_axis=0, tiled=True)
    grad_in = jnp.sum(received.astype(jnp.float32), axis=0).astype(jnp.bfloat16)
    return (grad_in, grad_up, grad_down)

def solution(mesh):
    gathers = mesh.shape["seq"] == 4 and mesh.shape["tensor"] == 8
    return jax.shard_map(
        local_all_tokens if gathers else local,
        mesh=mesh,
        in_specs=(
            P(("seq", "tensor"), None),
            P(("seq", "tensor"), None),
            P("tensor", None, None, None),
            P("tensor", None),
            P("tensor", None, None, None),
            P("tensor", None),
        ),
        out_specs=(
            P(("seq", "tensor"), None),
            P("tensor", None, "seq", None),
            P("tensor", None, "seq", None),
        ),
        check_vma=False,
    )
```
